256 devices in a mesh: mem: 8 (over y, core), tile: 32 (over z, x).
Axes of the slice: x: 4, y: 4, z: 8, core: 2. Of those that a mesh axis runs over, the one named last changes fastest.
Arguments:
- members: bfloat16 [8, 8, 1024, 2048], P('mem', None, 'tile'), may hold values from -6 to 6
- increment: float32 [8, 1024, 2048], P('mem', 'tile'), may hold values from -6 to 6
- weights: float32 [16], replicated, may hold values from 0.25 to 4
Outputs:
- applied: float32 [8, 1024, 2048], P('mem', 'tile')
The draws below stay inside these ranges and needn't reach their ends.
All inputs are finite; a program needn't handle non-finite values.
Results may differ from the reference program's by a relative error of at most 0.0017.
Values may be sent and summed in bfloat16 or wider, within the bound.
A program may use at most 64 MiB of HBM per device.

```python
import math
import jax
import jax.numpy as jnp
from jax import lax

NX = 2048
LEV = 8
LVLS = 5
NY = 1024
MEMBERS = 8
WEIGHTS = 16


def level_of(own_key, extent, split, smallest, high):
    factor_of = 1.0
    for position, blocks in split:
        heights = jax.random.uniform(jax.random.fold_in(jax.random.fold_in(own_key, 6), position), (blocks,), jnp.float32, smallest / len(split), high / len(split))
        factor_of = factor_of * jnp.repeat(jnp.exp(heights), extent[position] // blocks).reshape((-1,) + (1,) * (len(extent) - 1 - position))
    return factor_of


def gaussian(own_key, shape, spread, most, split=(), dtype=jnp.bfloat16):
    values = jax.random.normal(own_key, shape, jnp.float32) * spread
    if len(split) > 0:
        values = level_of(own_key, shape, split, -0.22, 0.18) * values
    return jnp.clip(values, min=-most, max=most).astype(dtype)


def setup_inputs(seed: int = 0) -> dict:
    keys = jax.random.split(jax.random.key(seed), 4)
    members = gaussian(keys[0], (MEMBERS, LEV, NY, NX), 1.0, 6.0, ((0, 8), (2, 32)))
    increment = gaussian(keys[1], (LEV, NY, NX), 1.0, 6.0, ((0, 8), (1, 32)), jnp.float32)
    weights = jnp.clip(jnp.exp(jax.random.uniform(keys[2], (WEIGHTS,), jnp.float32, math.log(0.25), math.log(4.0))), 0.25, 4.0)
    return {"members": members, "increment": increment, "weights": weights}


lift_first = -1.586134342059924
lift_second = -0.052980118572961
lift_third = 0.882911075530934
lift_fourth = 0.443506852043971
scale_kappa = 1.149604398860241


def forward_lift(even_part, odd_part, step_after, step_before):
    odd_part = odd_part + lift_first * (even_part + step_after(even_part))
    even_part = even_part + lift_second * (step_before(odd_part) + odd_part)
    odd_part = odd_part + lift_third * (even_part + step_after(even_part))
    even_part = even_part + lift_fourth * (step_before(odd_part) + odd_part)
    return even_part * scale_kappa, odd_part / scale_kappa


def inverse_lift(low_part, high_part, step_after, step_before):
    even_part = low_part / scale_kappa
    odd_part = high_part * scale_kappa
    even_part = even_part - lift_fourth * (step_before(odd_part) + odd_part)
    odd_part = odd_part - lift_third * (even_part + step_after(even_part))
    even_part = even_part - lift_second * (step_before(odd_part) + odd_part)
    odd_part = odd_part - lift_first * (even_part + step_after(even_part))
    return even_part, odd_part


def roll_next_rows(values):
    return jnp.roll(values, -1, axis=1)


def roll_prior_rows(values):
    return jnp.roll(values, 1, axis=1)


def column_next(values):
    return jnp.roll(values, -1, axis=-1)


def column_prior(values):
    return jnp.roll(values, 1, axis=-1)


def split_columns(values):
    return forward_lift(values[..., 0::2], values[..., 1::2], column_next, column_prior)


def join_columns(low_part, high_part):
    even_part, odd_part = inverse_lift(low_part, high_part, column_next, column_prior)
    merged = jnp.stack((even_part, odd_part), axis=-1)
    return merged.reshape(even_part.shape[:-1] + (2 * even_part.shape[-1],))


def analysis_level(approx, step_after, step_before):
    low_rows, high_rows = forward_lift(approx[:, 0::2], approx[:, 1::2], step_after, step_before)
    low_low, low_high = split_columns(low_rows)
    high_low, high_high = split_columns(high_rows)
    return low_low, jnp.stack((low_high, high_low, high_high), axis=1)


def synthesis_level(approx, detail, step_after, step_before):
    low_rows = join_columns(approx, detail[:, 0])
    high_rows = join_columns(detail[:, 1], detail[:, 2])
    even_part, odd_part = inverse_lift(low_rows, high_rows, step_after, step_before)
    merged = jnp.stack((even_part, odd_part), axis=2)
    return merged.reshape((merged.shape[0], 2 * merged.shape[1], merged.shape[3]))


def analyze_levels(approx, level_count, step_after, step_before):
    details = []
    for level_index in range(level_count):
        approx, detail = analysis_level(approx, step_after, step_before)
        details.append(detail)
    return approx, tuple(details)


def synthesize(approx, details, step_after, step_before):
    for detail in reversed(details):
        approx = synthesis_level(approx, detail, step_after, step_before)
    return approx


def reference(members, increment, weights):
    initial = (jnp.zeros((LEV, NY // 2 ** LVLS, NX // 2 ** LVLS), jnp.float32),)
    initial = initial + tuple(jnp.zeros((LEV, 3, NY // 2 ** (level_index + 1), NX // 2 ** (level_index + 1)), jnp.float32) for level_index in range(LVLS))

    def accumulate(totals, member):
        approx, details = analyze_levels(member.astype(jnp.float32), LVLS, roll_next_rows, roll_prior_rows)
        squares = (approx * approx,) + tuple(detail * detail for detail in details)
        return tuple(running + square for running, square in zip(totals, squares)), None

    energy, unused = lax.scan(accumulate, initial, members)
    own_approx, own_details = analyze_levels(increment, LVLS, roll_next_rows, roll_prior_rows)
    scale_members = 1.0 / (MEMBERS - 1)
    product_approx = (weights[3 * LVLS] * scale_members) * energy[0] * own_approx
    products = tuple((weights[3 * level_index:3 * level_index + 3] * scale_members).reshape((1, 3, 1, 1)) * energy[level_index + 1] * own_details[level_index] for level_index in range(LVLS))
    return synthesize(product_approx, products, roll_next_rows, roll_prior_rows)
```

```python
import functools

import jax
import jax.numpy as jnp
import numpy as np
from jax import lax
from jax.experimental import pallas as pl
from jax.experimental.pallas import tpu as pltpu
from jax.sharding import PartitionSpec as P

f32, bf16 = jnp.float32, jnp.bfloat16
MESH = pl.DeviceIdType.MESH
LIFT = (-1.586134342059924, -0.052980118572961, 0.882911075530934, 0.443506852043971)
KAPPA = 1.149604398860241
NROW, BAND, LEVELS, MEM, TILE = 1024, 32, 8, 8, 32
RANK = (2, 3, 4)


def forward_matrix(n):
    x = np.eye(n)
    e, o = x[0::2], x[1::2]
    after = lambda v: np.roll(v, -1, 0)
    before = lambda v: np.roll(v, 1, 0)
    o = o + LIFT[0] * (e + after(e))
    e = e + LIFT[1] * (before(o) + o)
    o = o + LIFT[2] * (e + after(e))
    e = e + LIFT[3] * (before(o) + o)
    return e * KAPPA, o / KAPPA


def inverse_matrix(n):
    z = np.eye(n)
    e, o = z[: n // 2] / KAPPA, z[n // 2 :] * KAPPA
    after = lambda v: np.roll(v, -1, 0)
    before = lambda v: np.roll(v, 1, 0)
    e = e - LIFT[3] * (before(o) + o)
    o = o - LIFT[2] * (e + after(e))
    e = e - LIFT[1] * (before(o) + o)
    o = o - LIFT[0] * (e + after(e))
    out = np.zeros((n, n))
    out[0::2], out[1::2] = e, o
    return out


def pieces(m):
    hi = np.asarray(m, np.float32).astype(bf16)
    lo = (np.asarray(m, np.float64) - hi.astype(np.float64)).astype(bf16)
    return hi, lo


def three(m):
    hi, lo = pieces(m)
    return np.concatenate([hi, hi, lo], axis=1)


def two(m):
    hi, lo = pieces(m)
    return np.concatenate([hi, lo], axis=1)


def per_field(m, fields, places=None):
    return np.kron(np.eye(fields), m)


def pad_rows(m, rows):
    return np.concatenate([m, np.zeros((rows - m.shape[0], m.shape[1]))], axis=0)


@functools.lru_cache(maxsize=None)
def constants():
    c = {}
    lows, highs, chain = [], [], np.eye(NROW)
    for k in range(5):
        low, high = forward_matrix(NROW >> k)
        lows.append(low @ chain)
        highs.append(high @ chain)
        chain = lows[-1]
    mid = 16

    def block(mat, k, d):
        r = (BAND >> k) // 2
        m = mat[mid * r : (mid + 1) * r, (mid - d) * BAND : (mid - d + 1) * BAND].copy()
        m[np.abs(m) < 1e-13] = 0.0
        return m

    lo2048, hi2048 = forward_matrix(2048)
    bf = np.concatenate([lo2048[512:640, 896:1408], hi2048[512:640, 896:1408]], axis=0).T
    c["bf_hi"], c["bf_lo"] = pieces(bf)
    l128, h128 = forward_matrix(128)
    c["b4_hi"], c["b4_lo"] = pieces(np.concatenate([l128, h128], axis=0).T)
    s2048 = inverse_matrix(2048)
    bi = np.concatenate([s2048[1024:1280, 384:768], s2048[1024:1280, 1024 + 384 : 1024 + 768]], axis=1).T
    c["bi_hi"], c["bi_lo"] = pieces(bi)
    c["i4_hi"], c["i4_lo"] = pieces(inverse_matrix(128).T)

    for k in range(3):
        bl, bh = {}, {}
        for d in (0, 1, -1):
            bl[d], bh[d] = block(lows[k], k, d), block(highs[k], k, d)
        r = RANK[k]
        rows_h = 16 >> k
        place = {}
        for part in ("h", "l"):
            for d in (1, -1):
                full = np.concatenate([bl[d], bh[d]], axis=0) if part == "h" else bh[d]
                u, s, vt = np.linalg.svd(full, full_matrices=False)
                assert s[r:].max(initial=0.0) < 1e-12
                place[part, d] = (u[:, :r] * s[:r], vt[:r])
        for f, tag in ((8, "m"), (1, "i")):
            if k < 2:
                own_h = np.concatenate([per_field(bl[0], f), per_field(bh[0], f)], axis=0)
                own_l = per_field(bh[0], f)
                uh = {d: np.concatenate([per_field(place["h", d][0][:rows_h], f), per_field(place["h", d][0][rows_h:], f)], axis=0) for d in (1, -1)}
                ul = {d: per_field(place["l", d][0], f) for d in (1, -1)}
            else:
                own_h = per_field(np.concatenate([bl[0], bh[0]], axis=0), f)
                top = lambda m: np.concatenate([m, 0 * m], axis=0)
                bot = lambda m: np.concatenate([0 * m, m], axis=0)
                own_l = np.stack([per_field(top(bh[0]), f), per_field(bot(bh[0]), f)])
                uh = {d: per_field(place["h", d][0], f) for d in (1, -1)}
                ul = {d: np.stack([per_field(top(place["l", d][0]), f), per_field(bot(place["l", d][0]), f)]) for d in (1, -1)}
            c[f"a{k}h{tag}"] = three(own_h)
            rows = 8 if f == 1 else 8 * 2 * r
            for d, name in ((1, "n"), (-1, "p")):
                vh, vl = per_field(place["h", d][1], f), per_field(place["l", d][1], f)
                if f == 1:
                    vh, vl = pad_rows(vh, 8), pad_rows(np.concatenate([0 * vh, vl], axis=0), 8)
                c[f"v{k}h{tag}{name}"], c[f"v{k}l{tag}{name}"] = three(vh), three(vl)
            cut = two if f == 8 else three

            def spread(u, at):
                out = []
                for d in (1, -1):
                    m = np.zeros((u[d].shape[0], rows))
                    m[:, at : at + u[d].shape[1]] = u[d]
                    out.append(m)
                return np.concatenate(out, axis=1)

            c[f"u{k}h{tag}"] = cut(spread(uh, 0))
            if k < 2:
                c[f"a{k}l{tag}"] = three(own_l)
                c[f"u{k}l{tag}"] = cut(spread(ul, f * r))
            else:
                for i in range(2):
                    c[f"a{k}l{i}{tag}"] = three(own_l[i])
                    c[f"u{k}l{i}{tag}"] = cut(spread({d: ul[d][i] for d in ul}, f * r))

    def tile34(d):
        z = np.zeros((8, 3 * BAND))
        z[0:1, :BAND], z[1:2, :BAND] = block(lows[4], 4, d), block(highs[4], 4, d)
        z[2:4, BAND : 2 * BAND] = block(lows[3], 3, d)
        z[4:6, BAND : 2 * BAND] = block(highs[3], 3, d)
        z[6:8, 2 * BAND :] = block(highs[3], 3, d)
        return z

    def tiles(z, f):
        return np.concatenate([per_field(z[:, i * BAND : (i + 1) * BAND], f) for i in range(3)], axis=1)

    for f, tag in ((8, "m"), (1, "i")):
        out = [tiles(tile34(d), f) for d in (0, 1, -1, 2, -2)]
        for d in (3, -3, 4):
            z = tile34(d)
            assert np.abs(z[2:]).max() == 0
            m = tiles(z[:2], f)
            out.append(m if f == 8 else pad_rows(m, 8))
        assert np.abs(tile34(-4)).max() == 0 and np.abs(tile34(5)).max() == 0 and np.abs(tile34(-5)).max() == 0
        c[f"w{tag}"] = three(np.concatenate(out, axis=0))
    spread = np.kron(np.eye(8), np.eye(8)[:, :2])
    spread = np.concatenate([spread, np.zeros((64, 8))], axis=1)
    spread = np.concatenate([spread, np.zeros((8, 24))], axis=0)
    spread[64:66, 16:18] = np.eye(2)
    spread = np.concatenate([spread, np.zeros((72, 8))], axis=1)
    c["x34"] = np.concatenate([spread, spread], axis=1).astype(bf16)

    def row_inverse(k, start, stop, rows_out, low_start, low_count, high_slots):
        n = NROW >> k
        m = inverse_matrix(n)
        m[np.abs(m) < 1e-13] = 0.0
        base = mid * (BAND >> k)
        part = m[base + start : base + stop]
        low, high = part[:, : n // 2], part[:, n // 2 :]
        half = base // 2
        out_low = np.zeros((rows_out, low_count))
        out_low[: stop - start] = low[:, half + low_start : half + low_start + low_count]
        assert np.abs(low).sum() - np.abs(out_low).sum() < 1e-9
        out_high = np.zeros((rows_out, len(high_slots)))
        for i, s in enumerate(high_slots):
            if s is not None:
                out_high[: stop - start, i] = high[:, half + s]
        assert np.abs(high).sum() - np.abs(out_high).sum() < 1e-9, k
        return out_low, out_high

    def pick(k, start, stop, rows_out, low_slots, high_slots):
        n = NROW >> k
        m = inverse_matrix(n)
        m[np.abs(m) < 1e-13] = 0.0
        base = mid * (BAND >> k)
        part = m[base + start : base + stop]
        low, high = part[:, : n // 2], part[:, n // 2 :]
        half = base // 2
        out = np.zeros((rows_out, len(low_slots)))
        seen = 0.0
        for i in range(len(low_slots)):
            if low_slots[i] is not None:
                out[: stop - start, i] += low[:, half + low_slots[i]]
            if high_slots[i] is not None:
                out[: stop - start, i] += high[:, half + high_slots[i]]
        want = (np.abs(low).sum() if any(s is not None for s in low_slots) else 0.0) + (
            np.abs(high).sum() if any(s is not None for s in high_slots) else 0.0
        )
        assert abs(want - np.abs(out).sum()) < 1e-9, k
        return out

    none = [None]
    bands = list(range(-3, 5))
    flat = lambda rows: sum(rows, [])
    l4 = flat([[b] + none * 7 for b in bands])
    h4 = flat([none + [b] + none * 6 for b in bands])
    c["s4"] = three(pick(4, -2, 6, 8, l4, h4))
    l3 = flat([none * 2 + [2 * b, 2 * b + 1] + none * 4 for b in bands])
    h3 = flat([none * 4 + [2 * b, 2 * b + 1] + none * 2 for b in bands])
    h3l = flat([none * 6 + [2 * b, 2 * b + 1] for b in bands])
    c["s3h"] = three(pick(3, -2, 8, 16, l3, h3))
    c["s3l"] = three(pick(3, -2, 8, 16, none * 64 + list(range(-2, 6)) + none * 8, h3l + none * 16))
    near = (-1, 0, 1)
    l2 = flat([[4 * b + i for i in range(4)] + none * 4 for b in near]) + none * 8
    h2 = flat([none * 4 + [4 * b + i for i in range(4)] for b in near]) + none * 8
    c["s2h"] = three(pick(2, -2, 12, 16, l2, h2))
    low_ext = [-2 + i if i < 10 else None for i in range(16)]
    ha = flat([[4 * b + i for i in range(4)] + none * 4 for b in near]) + none * 8
    hb = flat([none * 4 + [4 * b + i for i in range(4)] for b in near]) + none * 8
    c["s2l0"] = three(pick(2, -2, 12, 16, none * 32 + low_ext, ha + none * 16))
    c["s2l1"] = three(pick(2, -2, 12, 16, none * 32 + low_ext, hb + none * 16))
    s1 = list(range(8)) + list(range(-4, 0)) + list(range(8, 12))
    c["s1h"] = three(pick(1, -2, 18, 24, s1 + none * 16, none * 16 + s1))
    low_ext = [-2 + i if i < 14 else None for i in range(16)]
    c["s1l"] = three(pick(1, -2, 18, 24, low_ext + none * 16, none * 16 + s1))
    s0 = list(range(16)) + [-2, -1, 16, 17] + none * 4
    c["s0h"] = three(pick(0, 0, 32, 32, s0 + none * 24, none * 24 + s0))
    low_ext = [-2 + i if i < 20 else None for i in range(24)]
    c["s0l"] = three(pick(0, 0, 32, 32, low_ext + none * 24, none * 24 + s0))
    return c


def split(x):
    hi = x.astype(bf16)
    return hi, (x - hi.astype(f32)).astype(bf16)


def dot(a, b):
    return jnp.dot(a, b, preferred_element_type=f32)


def rows(*parts):
    return jnp.concatenate(parts, axis=0)


def lanes(*parts):
    return jnp.concatenate(parts, axis=1)


def left(matrix, x):
    hi, lo = split(x)
    return dot(matrix, rows(hi, lo, hi))


NAMES = tuple(sorted(constants()))


def kernel(*refs):
    members, increment, weights = refs[:3]
    c = dict(zip(NAMES, refs[3 : 3 + len(NAMES)]))
    out = refs[3 + len(NAMES)]
    (t_hi, t_lo, u_hi, u_lo, y0, y1, yc, i0, i1, ic,
     hs0, hs1, hs2, hr0, hr1, hr2, gs0, gs1, gs2, gr0, gr1, gr2, ks, kr, qs, qr,
     e0, e1, ce0, ce1, es0, es1, er0, er1, p0, p1, pc, ss0, ss1, sr0, sr1, syc, srt,
     sem_s, sem_r) = refs[4 + len(NAMES):]
    mem, tile = lax.axis_index("mem"), lax.axis_index("tile")
    ypos, core = lax.div(mem, 2), lax.rem(mem, 2)

    def at_tile(d):
        return (mem, lax.rem(tile + TILE + d, TILE))

    def at_y(j):
        return (lax.rem(ypos + j, 4) * 2 + core, tile)

    partner = (ypos * 2 + 1 - core, tile)
    near = [at_tile(d) for d in (1, -1, 2, -2, 3, -3, 4, -4)] + [partner] + [at_y(j) for j in (1, 2, 3)]
    barrier = pltpu.get_barrier_semaphore()
    for device in near:
        pl.semaphore_signal(barrier, inc=1, device_id=device, device_id_type=MESH)

    sent = []

    def send(src, dst, device):
        n = len(sent)
        copy = pltpu.make_async_remote_copy(
            src_ref=src, dst_ref=dst, send_sem=sem_s.at[n], recv_sem=sem_r.at[n], device_id=device, device_id_type=MESH
        )
        copy.start()
        sent.append(copy)
        return copy

    bf_hi, bf_lo = c["bf_hi"], c["bf_lo"]

    def window(ref, width, j, first, last):
        start = 256 * j - 128
        tiles = [(start // 128 + i) % (width // 128) for i in range(4)]
        groups = []
        for t in tiles:
            if groups and groups[-1][1] == t:
                groups[-1][1] = t + 1
            else:
                groups.append([t, t + 1])
        return lanes(*[ref[first:last, 128 * a : 128 * b] for a, b in groups]) if len(groups) > 1 else ref[first:last, 128 * groups[0][0] : 128 * groups[0][1]]

    def put(hi_ref, lo_ref, first, last, width, j, r):
        hi, lo = split(r)
        half = width // 2
        for ref, v in ((hi_ref, hi), (lo_ref, lo)):
            ref[first:last, 128 * j : 128 * j + 128] = v[:, :128]
            ref[first:last, half + 128 * j : half + 128 * j + 128] = v[:, 128:]

    m_all = members
    inc = increment[...]
    inc_hi, inc_lo = split(inc)
    for j in range(8):
        w = window(m_all, 2048, j, 0, 256)
        put(t_hi, t_lo, 0, 256, 2048, j, dot(w, bf_hi[...]) + dot(w, bf_lo[...]))
    u_hi[...] = inc_hi
    u_lo[...] = inc_lo
    for j in range(8):
        a, b = window(u_hi, 2048, j, 0, 32), window(u_lo, 2048, j, 0, 32)
        put(t_hi, t_lo, 256, 288, 2048, j, dot(a, bf_hi[...]) + dot(b, bf_hi[...]) + dot(a, bf_lo[...]))

    base = [0, 2048, 3072, 3584, 3840]

    def part(k, which, first, last):
        half = 1024 >> k
        s = base[k] + (half if which == "h" else 0)
        hi, lo = t_hi[first:last, s : s + half], t_lo[first:last, s : s + half]
        return rows(hi, lo, hi)

    def halo(k, hs, hr, gs, gr):
        copies = []
        for n, (name, d) in enumerate((("n", 1), ("p", -1))):
            h = rows(dot(c[f"v{k}hm{name}"][...], part(k, "h", 0, 256)), dot(c[f"v{k}lm{name}"][...], part(k, "l", 0, 256)))
            hs[n] = h.astype(bf16)
            if not sent:
                pl.semaphore_wait(barrier, len(near))
            copies.append(send(hs.at[n], hr.at[n], at_tile(d)))
            gs[n] = dot(c[f"v{k}hi{name}"][...], part(k, "h", 256, 288)) + dot(c[f"v{k}li{name}"][...], part(k, "l", 256, 288))
            copies.append(send(gs.at[n], gr.at[n], at_tile(d)))
        return copies

    halos = [halo(0, hs0, hr0, gs0, gr0)]
    for k in range(1, 5):
        width = 2048 >> k
        src = base[k - 1]
        if k < 4:
            for j in range(max(width // 256, 1)):
                a = window(t_hi.at[:, src : src + width], width, j, 0, 288)
                b = window(t_lo.at[:, src : src + width], width, j, 0, 288)
                r = dot(a, bf_hi[...]) + dot(b, bf_hi[...]) + dot(a, bf_lo[...])
                put(t_hi.at[:, base[k] : base[k] + width], t_lo.at[:, base[k] : base[k] + width], 0, 288, width, j, r)
        else:
            a, b = t_hi[:, src : src + 128], t_lo[:, src : src + 128]
            r = dot(a, c["b4_hi"][...]) + dot(b, c["b4_hi"][...]) + dot(a, c["b4_lo"][...])
            hi, lo = split(r)
            t_hi[:, base[4] : base[4] + 128] = hi
            t_lo[:, base[4] : base[4] + 128] = lo
        if k == 1:
            halos.append(halo(1, hs1, hr1, gs1, gr1))
        if k == 2:
            halos.append(halo(2, hs2, hr2, gs2, gr2))

    def stack34(first, last):
        hi = rows(*[t_hi[first:last, s : s + 128] for s in (base[4], base[3] + 128, base[3])])
        lo = rows(*[t_lo[first:last, s : s + 128] for s in (base[4], base[3] + 128, base[3])])
        return rows(hi, lo, hi)

    wm = dot(c["wm"][...], stack34(0, 256))
    wi = dot(c["wi"][...], stack34(256, 288))
    yc[:, 384:] = wm[0:64]
    ic[:, 384:] = wi[0:8]
    far = []
    for n, d in enumerate((1, -1, 2, -2)):
        ks[n] = rows(wm[64 + 64 * n : 128 + 64 * n], wi[8 + 8 * n : 16 + 8 * n])
        far.append(send(ks.at[n], kr.at[n], at_tile(d)))
    for n, d in enumerate((3, -3, 4)):
        qs[n] = rows(wm[320 + 16 * n : 336 + 16 * n], wi[40 + 8 * n : 48 + 8 * n])
        far.append(send(qs.at[n], qr.at[n], at_tile(d)))

    y = dot(c["a0hm"][...], part(0, "h", 0, 256))
    y0[:, 0:1024], y0[:, 1024:2048] = y[:128], y[128:]
    y0[:, 2048:] = dot(c["a0lm"][...], part(0, "l", 0, 256))
    y = dot(c["a0hi"][...], part(0, "h", 256, 288))
    i0[:, 0:1024], i0[:, 1024:2048] = y[:16], y[16:]
    i0[:, 2048:] = dot(c["a0li"][...], part(0, "l", 256, 288))
    y = dot(c["a1hm"][...], part(1, "h", 0, 256))
    y1[:, 0:512], y1[:, 512:1024] = y[:64], y[64:]
    y1[:, 1024:] = dot(c["a1lm"][...], part(1, "l", 0, 256))
    y = dot(c["a1hi"][...], part(1, "h", 256, 288))
    i1[:, 0:512], i1[:, 512:1024] = y[:8], y[8:]
    i1[:, 1024:] = dot(c["a1li"][...], part(1, "l", 256, 288))
    for ref, tag, first, last in ((yc, "m", 0, 256), (ic, "i", 256, 288)):
        ref[:, 0:256] = dot(c[f"a2h{tag}"][...], part(2, "h", first, last))
        p = part(2, "l", first, last)
        ref[:, 256:384] = dot(c[f"a2l0{tag}"][...], p[:, :128]) + dot(c[f"a2l1{tag}"][...], p[:, 128:])

    def got(ref):
        a, b = ref[0], ref[1]
        return rows(a, b, a, b)

    def got_inc(ref):
        hi, lo = split(rows(ref[0], ref[1]))
        return rows(hi, lo, hi)

    for copy in halos[0]:
        copy.wait_recv()
    g = got(hr0)
    q = dot(c["u0hm"][...], g)
    v = y0[:, 0:1024] + q[:128]
    e0[:, :, :, 0:1024] = (v * v).reshape(4, 2, 16, 1024)
    v = y0[:, 1024:2048] + q[128:]
    e0[:, :, :, 1024:2048] = (v * v).reshape(4, 2, 16, 1024)
    v = y0[:, 2048:] + dot(c["u0lm"][...], g)
    e0[:, :, :, 2048:] = (v * v).reshape(4, 2, 16, 1024)
    pair0 = send(e0.at[:, 1 - core], ce0, partner)

    for copy in halos[1]:
        copy.wait_recv()
    g = got(hr1)
    q = dot(c["u1hm"][...], g)
    v = y1[:, 0:512] + q[:64]
    e1[:, :, :, 0:512] = (v * v).reshape(4, 2, 8, 512)
    v = y1[:, 512:1024] + q[64:]
    e1[:, :, :, 512:1024] = (v * v).reshape(4, 2, 8, 512)
    v = y1[:, 1024:] + dot(c["u1lm"][...], g)
    e1[:, :, :, 1024:1536] = (v * v).reshape(4, 2, 8, 512)
    for copy in halos[2]:
        copy.wait_recv()
    g = got(hr2)
    v = yc[:, 0:256] + dot(c["u2hm"][...], g)
    e1[:, :, :, 1536:1792] = (v * v).reshape(4, 2, 8, 256)
    v = yc[:, 256:384] + dot(c["u2l0m"][...], g[:, :128]) + dot(c["u2l1m"][...], g[:, 128:])
    e1[:, :, :, 1792:1920] = (v * v).reshape(4, 2, 8, 128)
    for copy in far:
        copy.wait_recv()
    hi, lo = split(rows(qr[0] + qr[1] + qr[2], jnp.zeros((8, 128), f32)))
    v34 = kr[0] + kr[1] + kr[2] + kr[3] + dot(c["x34"][...], rows(hi, lo))
    v = yc[:, 384:] + v34[:64]
    e1[:, :, :, 1920:] = (v * v).reshape(4, 2, 8, 128)
    pair1 = send(e1.at[:, 1 - core], ce1, partner)

    g = got_inc(gr0)
    q = dot(c["u0hi"][...], g)
    i0[:, 0:1024] += q[:16]
    i0[:, 1024:2048] += q[16:]
    i0[:, 2048:] += dot(c["u0li"][...], g)
    g = got_inc(gr1)
    q = dot(c["u1hi"][...], g)
    i1[:, 0:512] += q[:8]
    i1[:, 512:1024] += q[8:]
    i1[:, 1024:] += dot(c["u1li"][...], g)
    g = got_inc(gr2)
    ic[:, 0:256] += dot(c["u2hi"][...], g)
    ic[:, 256:384] += dot(c["u2l0i"][...], g[:, :128]) + dot(c["u2l1i"][...], g[:, 128:])
    ic[:, 384:] += v34[64:72]

    pair0.wait_recv()
    over0 = []
    for j in (2, 1, 3):
        q = lax.rem(ypos + j, 4)
        both = e0[q, core] + ce0[q]
        es0[j - 1] = (both * both).astype(bf16)
        over0.append(send(es0.at[j - 1], er0.at[j - 1], at_y(j)))
    pair1.wait_recv()
    over1 = []
    for j in (2, 1, 3):
        q = lax.rem(ypos + j, 4)
        es1[j - 1] = e1[q, core] + ce1[q]
        over1.append(send(es1.at[j - 1], er1.at[j - 1], at_y(j)))
    own0 = e0[ypos, core] + ce0[ypos]
    own1 = e1[ypos, core] + ce1[ypos]

    w = [weights[i] * (1.0 / (MEM - 1)) for i in range(16)]
    for copy in over0:
        copy.wait_recv()
    energy = own0 + jnp.sqrt(er0[0].astype(f32)) + jnp.sqrt(er0[1].astype(f32)) + jnp.sqrt(er0[2].astype(f32))
    p0[:, 0:1024] = w[0] * energy[:, 0:1024] * i0[:, 0:1024]
    p0[:, 1024:2048] = w[2] * energy[:, 1024:2048] * i0[:, 1024:2048]
    p0[:, 2048:] = w[1] * energy[:, 2048:] * i0[:, 2048:]
    ss0[0] = p0[14:16]
    ss0[1] = p0[0:2]
    syn0 = [send(ss0.at[n], sr0.at[n], at_tile(d)) for n, d in enumerate((1, -1))]

    for copy in over1:
        copy.wait_recv()
    energy = own1 + er1[0] + er1[1] + er1[2]
    row = lax.broadcasted_iota(jnp.int32, (8, 128), 0)
    lane = lax.broadcasted_iota(jnp.int32, (8, 128), 1)
    w34 = jnp.where(
        row < 2,
        jnp.where(row == 0, jnp.where(lane < 64, w[15], w[12]), jnp.where(lane < 64, w[13], w[14])),
        jnp.where(row < 4, w[9], jnp.where(row < 6, w[11], w[10])),
    )
    w2 = jnp.where(lax.broadcasted_iota(jnp.int32, (8, 256), 0) < 4, w[6], w[8])
    pc[:, 0:256] = w2 * energy[:, 1536:1792] * ic[:, 0:256]
    pc[:, 256:384] = w[7] * energy[:, 1792:1920] * ic[:, 256:384]
    pc[:, 384:] = w34 * energy[:, 1920:] * ic[:, 384:]
    sync = [send(pc, syc.at[n], at_tile(d)) for n, d in enumerate((1, -1))]
    synt = [send(pc.at[:, 384:], srt.at[n], at_tile(d)) for n, d in enumerate((2, -2, 3, -3, -4))]
    p1[:, 0:512] = w[0 + 3] * energy[:, 0:512] * i1[:, 0:512]
    p1[:, 512:1024] = w[2 + 3] * energy[:, 512:1024] * i1[:, 512:1024]
    p1[:, 1024:] = w[1 + 3] * energy[:, 1024:1536] * i1[:, 1024:]
    ss1[0] = p1[4:8]
    ss1[1] = p1[0:4]
    syn1 = [send(ss1.at[n], sr1.at[n], at_tile(d)) for n, d in enumerate((1, -1))]

    for copy in synt + sync:
        copy.wait_recv()
    t = {-2: srt[0], 2: srt[1], -3: srt[2], 3: srt[3], 4: srt[4], 0: pc[:, 384:], -1: syc[0, :, 384:], 1: syc[1, :, 384:]}
    stack = rows(*[t[b] for b in range(-3, 5)])
    x = left(c["s4"][...], stack)
    hi, lo = split(x)
    ll3 = dot(hi, c["i4_hi"][...]) + dot(lo, c["i4_hi"][...]) + dot(hi, c["i4_lo"][...])
    x = lanes(left(c["s3l"][...], rows(stack, ll3, jnp.zeros((8, 128), f32))), left(c["s3h"][...], stack))

    bi_hi, bi_lo = c["bi_hi"], c["bi_lo"]

    def columns(x):
        half = x.shape[1] // 2
        hi, lo = split(x)
        outs = []
        count = half // 128

        def win(v, j):
            return lanes(*[v[:, s + 128 * ((j + i) % count) : s + 128 * ((j + i) % count) + 128] for s in (0, half) for i in (-1, 0, 1)])

        for j in range(count):
            a, b = win(hi, j), win(lo, j)
            outs.append(dot(a, bi_hi[...]) + dot(b, bi_hi[...]) + dot(a, bi_lo[...]))
        return lanes(*outs) if count > 1 else outs[0]

    ll2 = columns(x)
    z = jnp.zeros((8, 384), f32)
    stack = rows(syc[0, :, 0:384], pc[:, 0:384], syc[1, :, 0:384], z)
    x = lanes(
        left(c["s2l0"][...], rows(stack[:, 256:384], ll2[:, :128])),
        left(c["s2l1"][...], rows(stack[:, 256:384], ll2[:, 128:])),
        left(c["s2h"][...], stack[:, :256]),
    )
    ll1 = columns(x)
    for copy in syn1:
        copy.wait_recv()
    stack = rows(p1[...], sr1[0], sr1[1])
    x = lanes(
        left(c["s1l"][...], rows(ll1, stack[:, 1024:])),
        left(c["s1h"][...], rows(stack[:, 0:512], stack[:, 512:1024])),
    )
    ll0 = columns(x)
    for copy in syn0:
        copy.wait_recv()
    stack = rows(p0[...], sr0[0], sr0[1], jnp.zeros((4, 3072), f32))
    x = lanes(
        left(c["s0l"][...], rows(ll0, stack[:, 2048:])),
        left(c["s0h"][...], rows(stack[:, 0:1024], stack[:, 1024:2048])),
    )
    out[...] = columns(x)
    for copy in sent:
        copy.wait_send()


def local(members, increment, weights):
    c = constants()
    vmem = pl.BlockSpec(memory_space=pltpu.VMEM)
    v = pltpu.VMEM
    scratch = [
        v((288, 3968), bf16), v((288, 3968), bf16), v((32, 2048), bf16), v((32, 2048), bf16),
        v((128, 3072), f32), v((64, 1536), f32), v((64, 512), f32),
        v((16, 3072), f32), v((8, 1536), f32), v((8, 512), f32),
        v((2, 32, 1024), bf16), v((2, 48, 512), bf16), v((2, 64, 256), bf16),
        v((2, 32, 1024), bf16), v((2, 48, 512), bf16), v((2, 64, 256), bf16),
        v((2, 8, 1024), f32), v((2, 8, 512), f32), v((2, 8, 256), f32),
        v((2, 8, 1024), f32), v((2, 8, 512), f32), v((2, 8, 256), f32),
        v((4, 72, 128), f32), v((4, 72, 128), f32), v((3, 24, 128), f32), v((3, 24, 128), f32),
        v((4, 2, 16, 3072), f32), v((4, 2, 8, 2048), f32), v((4, 16, 3072), f32), v((4, 8, 2048), f32),
        v((3, 16, 3072), bf16), v((3, 8, 2048), f32), v((3, 16, 3072), bf16), v((3, 8, 2048), f32),
        v((16, 3072), f32), v((8, 1536), f32), v((8, 512), f32),
        v((2, 2, 3072), f32), v((2, 4, 1536), f32), v((2, 2, 3072), f32), v((2, 4, 1536), f32),
        v((2, 8, 512), f32), v((5, 8, 128), f32),
        pltpu.SemaphoreType.DMA((40,)), pltpu.SemaphoreType.DMA((40,)),
    ]
    result = pl.pallas_call(
        kernel,
        out_shape=jax.ShapeDtypeStruct((BAND, 2048), f32),
        in_specs=[vmem, vmem, pl.BlockSpec(memory_space=pltpu.SMEM)] + [vmem] * len(NAMES),
        out_specs=vmem,
        scratch_shapes=scratch,
        compiler_params=pltpu.CompilerParams(collective_id=0, has_side_effects=True, vmem_limit_bytes=56 * 2**20),
    )(members.reshape(256, 2048), increment.reshape(BAND, 2048), weights, *[jnp.asarray(c[n]) for n in NAMES])
    return result.reshape(1, BAND, 2048)


def solution(mesh):
    return jax.shard_map(
        local,
        mesh=mesh,
        in_specs=(P("mem", None, "tile", None), P("mem", "tile", None), P()),
        out_specs=P("mem", "tile", None),
        check_vma=False,
    )
```

```python
import functools

import jax
import jax.numpy as jnp
import numpy as np
from jax import lax
from jax.experimental import pallas as pl
from jax.experimental.pallas import tpu as pltpu
from jax.sharding import PartitionSpec as P

f32, bf16 = jnp.float32, jnp.bfloat16
MESH = pl.DeviceIdType.MESH
LIFT = (-1.586134342059924, -0.052980118572961, 0.882911075530934, 0.443506852043971)
KAPPA = 1.149604398860241
NROW, BAND, LEVELS, MEM, TILE = 1024, 32, 8, 8, 32
RANK = (2, 3, 4)


def forward_matrix(n):
    x = np.eye(n)
    e, o = x[0::2], x[1::2]
    after = lambda v: np.roll(v, -1, 0)
    before = lambda v: np.roll(v, 1, 0)
    o = o + LIFT[0] * (e + after(e))
    e = e + LIFT[1] * (before(o) + o)
    o = o + LIFT[2] * (e + after(e))
    e = e + LIFT[3] * (before(o) + o)
    return e * KAPPA, o / KAPPA


def inverse_matrix(n):
    z = np.eye(n)
    e, o = z[: n // 2] / KAPPA, z[n // 2 :] * KAPPA
    after = lambda v: np.roll(v, -1, 0)
    before = lambda v: np.roll(v, 1, 0)
    e = e - LIFT[3] * (before(o) + o)
    o = o - LIFT[2] * (e + after(e))
    e = e - LIFT[1] * (before(o) + o)
    o = o - LIFT[0] * (e + after(e))
    out = np.zeros((n, n))
    out[0::2], out[1::2] = e, o
    return out


def pieces(m):
    hi = np.asarray(m, np.float32).astype(bf16)
    lo = (np.asarray(m, np.float64) - hi.astype(np.float64)).astype(bf16)
    return hi, lo


def three(m):
    hi, lo = pieces(m)
    return np.concatenate([hi, hi, lo], axis=1)


def two(m):
    hi, lo = pieces(m)
    return np.concatenate([hi, lo], axis=1)


def per_field(m, fields, places=None):
    return np.kron(np.eye(fields), m)


def pad_rows(m, rows):
    return np.concatenate([m, np.zeros((rows - m.shape[0], m.shape[1]))], axis=0)


@functools.lru_cache(maxsize=None)
def constants():
    c = {}
    lows, highs, chain = [], [], np.eye(NROW)
    for k in range(5):
        low, high = forward_matrix(NROW >> k)
        lows.append(low @ chain)
        highs.append(high @ chain)
        chain = lows[-1]
    mid = 16

    def block(mat, k, d):
        r = (BAND >> k) // 2
        m = mat[mid * r : (mid + 1) * r, (mid - d) * BAND : (mid - d + 1) * BAND].copy()
        m[np.abs(m) < 1e-13] = 0.0
        return m

    def halves(m):
        return np.concatenate(pieces(m), axis=1)

    lo2048, hi2048 = forward_matrix(2048)
    bf = np.concatenate([lo2048[512:640, 896:1408], hi2048[512:640, 896:1408]], axis=0).T
    c["bf"] = np.concatenate(pieces(bf), axis=0)
    l128, h128 = forward_matrix(128)
    c["b4"] = np.concatenate(pieces(np.concatenate([l128, h128], axis=0).T), axis=0)
    s2048 = inverse_matrix(2048)
    bi = np.concatenate([s2048[1024:1280, 384:768], s2048[1024:1280, 1024 + 384 : 1024 + 768]], axis=1).T
    c["bi"] = np.concatenate(pieces(bi), axis=0)
    c["i4"] = np.concatenate(pieces(inverse_matrix(128).T), axis=0)

    inner, edge = list(range(4, 12)), [0, 1, 2, 3, 12, 13, 14, 15]
    for k in range(3):
        bl = {d: block(lows[k], k, d) for d in (0, 1, -1)}
        bh = {d: block(highs[k], k, d) for d in (0, 1, -1)}
        r = RANK[k]
        rows_h = 16 >> k
        place = {}
        for part in ("h", "l"):
            for d in (1, -1):
                full = np.concatenate([bl[d], bh[d]], axis=0) if part == "h" else bh[d]
                u, s, vt = np.linalg.svd(full, full_matrices=False)
                assert s[r:].max(initial=0.0) < 1e-12
                keep = s[:r] > 1e-12
                place[part, d] = (u[:, :r] * s[:r] * keep, vt[:r] * keep[:, None])
        top = lambda m: np.concatenate([m, 0 * m], axis=0)
        bot = lambda m: np.concatenate([0 * m, m], axis=0)
        for f, tag in ((8, "m"), (1, "i")):
            width = 8 * 2 * r if f == 8 else (4, 8, 8)[k]

            def sent(part):
                out = []
                for d in (1, -1):
                    v = place[part, d][1]
                    if f == 8:
                        out.append(per_field(v, f))
                    else:
                        out.append(pad_rows(np.concatenate([np.zeros((r if part == "l" else 0, BAND)), v], axis=0), 8))
                return out

            def spread(u, at):
                out = []
                for d in (1, -1):
                    m = np.zeros((u[d].shape[0], width))
                    m[:, at : at + u[d].shape[1]] = u[d]
                    out.append(m)
                m = np.concatenate(out, axis=1)
                if f == 1 and m.shape[1] < 16:
                    m = np.concatenate([m, np.zeros((m.shape[0], 16 - m.shape[1]))], axis=1)
                return m

            at_l = f * r
            if k == 0:
                own_h = [per_field(m[rows_], f) for rows_ in (inner, edge) for m in (bl[0], bh[0])]
                own_l = [per_field(bh[0][rows_], f) for rows_ in (inner, edge)]
                uh = {d: np.concatenate([per_field(place["h", d][0][:16][edge], f), per_field(place["h", d][0][16:][edge], f)], axis=0) for d in (1, -1)}
                ul = {d: per_field(place["l", d][0][edge], f) for d in (1, -1)}
                full_h = {d: place["h", d][0] for d in (1, -1)}
                assert all(np.abs(full_h[d][:16][inner]).max() < 1e-12 and np.abs(full_h[d][16:][inner]).max() < 1e-12 for d in full_h)
            elif k == 1:
                own_h = [per_field(bl[0], f), per_field(bh[0], f)]
                own_l = [per_field(bh[0], f)]
                uh = {d: np.concatenate([per_field(place["h", d][0][:rows_h], f), per_field(place["h", d][0][rows_h:], f)], axis=0) for d in (1, -1)}
                ul = {d: per_field(place["l", d][0], f) for d in (1, -1)}
            else:
                own_h = [per_field(np.concatenate([bl[0], bh[0]], axis=0), f)]
                own_l = [per_field(top(bh[0]), f), per_field(bot(bh[0]), f)]
                uh = {d: per_field(place["h", d][0], f) for d in (1, -1)}
                ul = {d: np.concatenate([per_field(top(place["l", d][0]), f), per_field(bot(place["l", d][0]), f)], axis=0) for d in (1, -1)}
            if k == 0 and f == 8:
                for part in ("h", "l"):
                    n, p = place[part, 1][1], place[part, -1][1]
                    assert np.abs(n[:, :24]).max() < 1e-12 and np.abs(p[:, 8:]).max() < 1e-12
                    n, p = per_field(n[:, 24:], f), per_field(p[:, :8], f)
                    z = np.zeros_like(n)
                    c[f"v0{part}"] = halves(np.concatenate([np.concatenate([n, z], axis=1), np.concatenate([z, p], axis=1)], axis=0))
                c["a0h"], c["a0l"] = halves(np.concatenate(own_h, axis=0)), halves(np.concatenate(own_l, axis=0))
            else:
                cut = halves if f == 8 else three
                c[f"a{k}h" + tag * (f == 1)] = cut(np.concatenate(own_h + sent("h"), axis=0))
                c[f"a{k}l" + tag * (f == 1)] = cut(np.concatenate(own_l + sent("l"), axis=0))
            cut = two if f == 8 else three
            c[f"u{k}h" + tag * (f == 1)] = cut(spread(uh, 0))
            c[f"u{k}l" + tag * (f == 1)] = cut(spread(ul, at_l))

    def tile34(d):
        z = np.zeros((8, 3 * BAND))
        z[0:1, :BAND], z[1:2, :BAND] = block(lows[4], 4, d), block(highs[4], 4, d)
        z[2:4, BAND : 2 * BAND] = block(lows[3], 3, d)
        z[4:6, BAND : 2 * BAND] = block(highs[3], 3, d)
        z[6:8, 2 * BAND :] = block(highs[3], 3, d)
        return z

    def tiles(z, f):
        return np.concatenate([per_field(z[:, i * BAND : (i + 1) * BAND], f) for i in range(3)], axis=1)

    for f, tag in ((8, "m"), (1, "i")):
        out = [tiles(tile34(d), f) for d in (0, 1, -1, 2, -2)]
        for d in (3, -3, 4):
            z = tile34(d)
            assert np.abs(z[2:]).max() == 0
            m = tiles(z[:2], f)
            out.append(m if f == 8 else pad_rows(m, 8))
        assert np.abs(tile34(-4)).max() == 0 and np.abs(tile34(5)).max() == 0 and np.abs(tile34(-5)).max() == 0
        m = np.concatenate(out, axis=0)
        c[f"w{tag}"] = halves(m) if f == 8 else three(m)
    spread = np.zeros((72, 32))
    spread[:64, :16] = np.kron(np.eye(8), np.eye(8)[:, :2])
    spread[64:66, 16:18] = np.eye(2)
    c["x34"] = np.concatenate([spread, spread], axis=1).astype(bf16)

    def pick(k, start, stop, rows_out, low_slots, high_slots):
        n = NROW >> k
        m = inverse_matrix(n)
        m[np.abs(m) < 1e-13] = 0.0
        base = mid * (BAND >> k)
        part = m[base + start : base + stop]
        low, high = part[:, : n // 2], part[:, n // 2 :]
        half = base // 2
        out = np.zeros((rows_out, len(low_slots)))
        seen = 0.0
        for i in range(len(low_slots)):
            if low_slots[i] is not None:
                out[: stop - start, i] += low[:, half + low_slots[i]]
            if high_slots[i] is not None:
                out[: stop - start, i] += high[:, half + high_slots[i]]
        want = (np.abs(low).sum() if any(s is not None for s in low_slots) else 0.0) + (
            np.abs(high).sum() if any(s is not None for s in high_slots) else 0.0
        )
        assert abs(want - np.abs(out).sum()) < 1e-9, k
        return out


    none = [None]
    bands = list(range(-3, 5))
    flat = lambda rows: sum(rows, [])
    l4 = flat([[b] + none * 7 for b in bands])
    h4 = flat([none + [b] + none * 6 for b in bands])
    c["s4"] = three(pick(4, -2, 6, 8, l4, h4))
    l3 = flat([none * 2 + [2 * b, 2 * b + 1] + none * 4 for b in bands])
    h3 = flat([none * 4 + [2 * b, 2 * b + 1] + none * 2 for b in bands])
    h3l = flat([none * 6 + [2 * b, 2 * b + 1] for b in bands])
    c["s3h"] = three(pick(3, -2, 8, 16, l3, h3))
    c["s3l"] = three(pick(3, -2, 8, 16, none * 64 + list(range(-2, 6)) + none * 8, h3l + none * 16))
    near = (-1, 0, 1)
    l2 = flat([[4 * b + i for i in range(4)] + none * 4 for b in near]) + none * 8
    h2 = flat([none * 4 + [4 * b + i for i in range(4)] for b in near]) + none * 8
    c["s2h"] = three(pick(2, -2, 12, 16, l2, h2))
    low_ext = [-2 + i if i < 10 else None for i in range(16)]
    ha = flat([[4 * b + i for i in range(4)] + none * 4 for b in near]) + none * 8
    hb = flat([none * 4 + [4 * b + i for i in range(4)] for b in near]) + none * 8
    c["s2l0"] = three(pick(2, -2, 12, 16, none * 32 + low_ext, ha + none * 16))
    c["s2l1"] = three(pick(2, -2, 12, 16, none * 32 + low_ext, hb + none * 16))
    s1 = list(range(8)) + list(range(-4, 0)) + list(range(8, 12))
    c["s1h"] = three(pick(1, -2, 18, 24, s1 + none * 16, none * 16 + s1))
    low_ext = [-2 + i if i < 14 else None for i in range(16)]
    c["s1l"] = three(pick(1, -2, 18, 24, low_ext + none * 16, none * 16 + s1))
    s0 = inner + edge + [-2, -1, 16, 17] + none * 4
    c["s0h"] = three(pick(0, 0, 32, 32, s0 + none * 24, none * 24 + s0))
    low_ext = [-2 + i if i < 20 else None for i in range(24)]
    c["s0l"] = three(pick(0, 0, 32, 32, low_ext + none * 24, none * 24 + s0))
    return c


GROUPS = (
    ("bf",),
    ("v0h", "v0l", "b4", "a1h", "a1l", "a2h", "a2l"),
    ("wm",),
    ("a0h", "a0l"),
    ("a0hi", "a0li", "a1hi", "a1li", "a2hi", "a2li", "wi"),
    ("u0h", "u0l", "u1h", "u1l", "u2h", "u2l", "x34", "u0hi", "u0li", "u1hi", "u1li", "u2hi", "u2li"),
    ("i4", "s4", "s3h", "s3l", "s2h", "s2l0", "s2l1", "s1h", "s1l", "s0h", "s0l"),
    ("bi",),
)


@functools.lru_cache(maxsize=None)
def packed():
    c = constants()
    assert sorted(sum(GROUPS, ())) == sorted(c)
    arrays, where = [], {}
    for g, names in enumerate(GROUPS):
        wide = max(-(-c[n].shape[1] // 128) * 128 for n in names)
        parts, at = [], 0
        for n in names:
            m = c[n]
            tall = -(-m.shape[0] // 16) * 16
            full = np.zeros((tall, wide), bf16)
            full[: m.shape[0], : m.shape[1]] = m
            parts.append(full)
            where[n] = (g, at, m.shape[0], m.shape[1])
            at += tall
        arrays.append(np.concatenate(parts, axis=0))
    return arrays, where


def split(x):
    hi = x.astype(bf16)
    return hi, (x - hi.astype(f32)).astype(bf16)


def dot(a, b):
    return jnp.dot(a, b, preferred_element_type=f32)


def rows(*parts):
    return jnp.concatenate(parts, axis=0)


def lanes(*parts):
    return jnp.concatenate(parts, axis=1) if len(parts) > 1 else parts[0]


COUNT = len(GROUPS)


def kernel(members_hbm, increment_hbm, weights_hbm, *refs):
    groups_hbm, out, groups = refs[:COUNT], refs[COUNT], refs[COUNT + 1 : 2 * COUNT + 1]
    (members, increment, weights, t_hi, t_lo, b_hi, b_lo, u_hi, u_lo,
     y0i, y0e, y1, yc, i0i, i0e, i1, ic,
     hs0, hs1, hs2, hr0, hr1, hr2, gs0, gs1, gs2, gr0, gr1, gr2,
     ks, kr, js, jr, qs, qr,
     e0i, e0e, e1, ce0i, ce0e, ce1, es0i, es0e, es1, es2, er0i, er0e, er1, er2,
     p0i, p0e, p1, pc, ss0, ss1, sr0, sr1, syc, srt,
     sem_s, sem_r, sem_l) = refs[2 * COUNT + 1 :]
    where = packed()[1]
    mem, tile = lax.axis_index("mem"), lax.axis_index("tile")
    ypos, core = lax.div(mem, 2), lax.rem(mem, 2)

    def at_tile(d):
        return (mem, lax.rem(tile + TILE + d, TILE))

    def at_y(j):
        return (lax.rem(ypos + j, 4) * 2 + core, tile)

    partner = (ypos * 2 + 1 - core, tile)
    near = [at_tile(d) for d in (1, -1, 2, -2, 3, -3, 4, -4)] + [partner] + [at_y(j) for j in (1, 2, 3)]
    barrier = pltpu.get_barrier_semaphore()
    for device in near:
        pl.semaphore_signal(barrier, inc=1, device_id=device, device_id_type=MESH)

    sources = [(groups_hbm[0], groups[0]), (members_hbm, members), (increment_hbm, increment)]
    sources += [(groups_hbm[g], groups[g]) for g in range(1, COUNT)] + [(weights_hbm, weights)]
    loads = [pltpu.make_async_copy(a, b, sem_l.at[n]) for n, (a, b) in enumerate(sources)]
    for load in loads:
        load.start()
    order = [0] + list(range(3, COUNT + 2))
    loaded = set()

    def need(n):
        if n not in loaded:
            loads[n].wait()
            loaded.add(n)

    def const(name):
        g, at, tall, wide = where[name]
        need(order[g])
        return groups[g][at : at + tall, :wide]

    def triple(name):
        m = const(name)
        half = m.shape[1] // 2
        return lanes(m[:, :half], m[:, :half], m[:, half:])

    sent = []

    def send(src, dst, device):
        n = len(sent)
        if n == 0:
            pl.semaphore_wait(barrier, len(near))
        copy = pltpu.make_async_remote_copy(
            src_ref=src, dst_ref=dst, send_sem=sem_s.at[n], recv_sem=sem_r.at[n], device_id=device, device_id_type=MESH
        )
        copy.start()
        sent.append(copy)
        return copy

    def window(ref, width, j, first, last):
        start = 256 * j - 128
        groups_ = []
        for t in [(start // 128 + i) % (width // 128) for i in range(4)]:
            if groups_ and groups_[-1][1] == t:
                groups_[-1][1] = t + 1
            else:
                groups_.append([t, t + 1])
        return lanes(*[ref[first:last, 128 * a : 128 * b] for a, b in groups_])

    def put(hi_ref, lo_ref, first, last, width, j, r):
        half = width // 2
        for ref, v in zip((hi_ref, lo_ref), split(r)):
            ref[first:last, 128 * j : 128 * j + 128] = v[:, :128]
            ref[first:last, half + 128 * j : half + 128 * j + 128] = v[:, 128:]

    base = [0, 2048, 3072, 3584, 3840]
    bf = const("bf")
    bf_hi, bf_lo = bf[:512], bf[512:]
    need(1)
    for j in range(8):
        w = window(members, 2048, j, 0, 256)
        r = dot(w, bf_hi) + dot(w, bf_lo)
        put(t_hi, t_lo, 0, 256, 2048, j, r)
        r = r.reshape(8, 32, 256)
        put(b_hi, b_lo, 0, 128, 2048, j, rows(r[:, 24:].reshape(64, 256), r[:, :8].reshape(64, 256)))

    def part(k, which, first, last):
        half = 1024 >> k
        s = base[k] + (half if which == "h" else 0)
        hi, lo = t_hi[first:last, s : s + half], t_lo[first:last, s : s + half]
        return rows(hi, lo, hi)

    owed = {}
    for which, s in (("h", 1024), ("l", 0)):
        hi, lo = b_hi[:, s : s + 1024], b_lo[:, s : s + 1024]
        owed[which] = dot(triple("v0" + which), rows(hi, lo, hi))
    halos = [[], [], []]

    def share(k, h, l, hs, hr):
        half = h.shape[0] // 2
        for n, d in enumerate((1, -1)):
            hs[n] = rows(h[n * half : n * half + half], l[n * half : n * half + half]).astype(bf16)
            halos[k].append(send(hs.at[n], hr.at[n], at_tile(d)))

    share(0, owed["h"], owed["l"], hs0, hr0)

    need(2)
    hi, lo = split(increment[...])
    u_hi[...], u_lo[...] = hi, lo
    a = rows(*[window(u_hi, 2048, j, 0, 32) for j in range(8)])
    b = rows(*[window(u_lo, 2048, j, 0, 32) for j in range(8)])
    r = dot(rows(a, b), bf_hi)
    r = r[:256] + r[256:] + dot(a, bf_lo)
    for j in range(8):
        put(t_hi, t_lo, 256, 288, 2048, j, r[32 * j : 32 * j + 32])

    def down(k):
        width, s = 2048 >> k, base[k - 1]
        if k < 4:
            for j in range(width // 256):
                a = window(t_hi.at[:, s : s + width], width, j, 0, 288)
                b = window(t_lo.at[:, s : s + width], width, j, 0, 288)
                r = dot(a, bf_hi) + dot(b, bf_hi) + dot(a, bf_lo)
                put(t_hi.at[:, base[k] : base[k] + width], t_lo.at[:, base[k] : base[k] + width], 0, 288, width, j, r)
        else:
            m = const("b4")
            a, b = t_hi[:, s : s + 128], t_lo[:, s : s + 128]
            hi, lo = split(dot(a, m[:128]) + dot(b, m[:128]) + dot(a, m[128:]))
            t_hi[:, base[4] : base[4] + 128] = hi
            t_lo[:, base[4] : base[4] + 128] = lo

    down(1)
    h = dot(triple("a1h"), part(1, "h", 0, 256))
    l = dot(triple("a1l"), part(1, "l", 0, 256))
    share(1, h[128:], l[64:], hs1, hr1)
    y1[:, 0:512], y1[:, 512:1024], y1[:, 1024:] = h[:64], h[64:128], l[:64]
    down(2)
    h = dot(triple("a2h"), part(2, "h", 0, 256))
    l = dot(triple("a2l"), part(2, "l", 0, 256))
    share(2, h[64:], l[128:], hs2, hr2)
    yc[:, 0:256], yc[:, 256:384] = h[:64], l[:64, :128] + l[64:128, 128:]
    down(3)
    down(4)

    def stack34(first, last):
        hi = rows(*[t_hi[first:last, s : s + 128] for s in (base[4], base[3] + 128, base[3])])
        lo = rows(*[t_lo[first:last, s : s + 128] for s in (base[4], base[3] + 128, base[3])])
        return rows(hi, lo, hi)

    wm = dot(triple("wm"), stack34(0, 256))
    wi = dot(const("wi"), stack34(256, 288))
    yc[:, 384:] = wm[0:64]
    ic[:, 384:] = wi[0:8]
    far = []
    for n, d in enumerate((1, -1)):
        ks[n] = rows(wm[64 + 64 * n : 128 + 64 * n], wi[8 + 8 * n : 16 + 8 * n])
        far.append(send(ks.at[n], kr.at[n], at_tile(d)))
    z8 = jnp.zeros((8, 128), f32)
    for n, d in enumerate((2, -2)):
        js[n] = rows(wm[192 + 64 * n : 256 + 64 * n], wi[24 + 8 * n : 32 + 8 * n], z8).astype(bf16)
        far.append(send(js.at[n], jr.at[n], at_tile(d)))
    for n, d in enumerate((3, -3, 4)):
        qs[n] = rows(wm[320 + 16 * n : 336 + 16 * n], wi[40 + 8 * n : 48 + 8 * n], z8).astype(bf16)
        far.append(send(qs.at[n], qr.at[n], at_tile(d)))

    y = dot(triple("a0h"), part(0, "h", 0, 256))
    x = dot(triple("a0l"), part(0, "l", 0, 256))
    for n, v in enumerate((y[:64], y[64:128], x[:64])):
        e0i[:, :, :, 1024 * n : 1024 * n + 1024] = (v * v).reshape(4, 2, 8, 1024)
    pair0i = send(e0i.at[:, 1 - core], ce0i, partner)
    y0e[:, 0:1024], y0e[:, 1024:2048], y0e[:, 2048:] = y[128:192], y[192:], x[64:]

    gifts = [[], [], []]

    def give(k, n8, p8, gs, gr):
        tall = gs.shape[1]
        for n, (d, v) in enumerate(((1, n8), (-1, p8))):
            gs[n] = v[:tall]
            gifts[k].append(send(gs.at[n], gr.at[n], at_tile(d)))

    y = dot(const("a0hi"), part(0, "h", 256, 288))
    x = dot(const("a0li"), part(0, "l", 256, 288))
    give(0, y[32:40] + x[16:24], y[40:48] + x[24:32], gs0, gr0)
    i0i[:, 0:1024], i0i[:, 1024:2048], i0i[:, 2048:] = y[:8], y[8:16], x[:8]
    i0e[:, 0:1024], i0e[:, 1024:2048], i0e[:, 2048:] = y[16:24], y[24:32], x[8:16]
    y = dot(const("a1hi"), part(1, "h", 256, 288))
    x = dot(const("a1li"), part(1, "l", 256, 288))
    give(1, y[16:24] + x[8:16], y[24:32] + x[16:24], gs1, gr1)
    i1[:, 0:512], i1[:, 512:1024], i1[:, 1024:] = y[:8], y[8:16], x[:8]
    y = dot(const("a2hi"), part(2, "h", 256, 288))
    x = dot(const("a2li"), part(2, "l", 256, 288))
    give(2, y[8:16] + x[16:24], y[16:24] + x[24:32], gs2, gr2)
    ic[:, 0:256], ic[:, 256:384] = y[:8], x[:8, :128] + x[8:16, 128:]

    def fold(v):
        half = v.shape[1] // 2
        v = v * v
        return rows(v[:, :half], v[:, half:]).astype(bf16)

    def unfold(v):
        v = jnp.sqrt(v.astype(f32))
        return lanes(v[:8], v[8:])

    def along_y(e, ce, es, er):
        copies = []
        for j in (2, 1, 3):
            q = lax.rem(ypos + j, 4)
            es[j - 1] = fold(e[q, core] + ce[q])
            copies.append(send(es.at[j - 1], er.at[j - 1], at_y(j)))
        return copies

    def total(e, ce, er, copies):
        v = e[ypos, core] + ce[ypos]
        for copy in copies:
            copy.wait_recv()
        return v + unfold(er[0]) + unfold(er[1]) + unfold(er[2])

    pair0i.wait_recv()
    over0i = along_y(e0i, ce0i, es0i, er0i)

    def got(k, ref):
        for copy in halos[k]:
            copy.wait_recv()
        a, b = ref[0], ref[1]
        return rows(a, b, a, b)

    g = got(0, hr0)
    q = dot(const("u0h"), g)
    x = dot(const("u0l"), g)
    for n, v in enumerate((q[:64], q[64:], x)):
        v = v + y0e[:, 1024 * n : 1024 * n + 1024]
        e0e[:, :, :, 1024 * n : 1024 * n + 1024] = (v * v).reshape(4, 2, 8, 1024)
    pair0e = send(e0e.at[:, 1 - core], ce0e, partner)

    g = got(1, hr1)
    q = dot(const("u1h"), g)
    x = dot(const("u1l"), g)
    for n, v in enumerate((q[:64], q[64:], x)):
        v = v + y1[:, 512 * n : 512 * n + 512]
        e1[:, :, :, 512 * n : 512 * n + 512] = (v * v).reshape(4, 2, 8, 512)
    g = got(2, hr2)
    v = yc[:, 0:256] + dot(const("u2h"), g)
    e1[:, :, :, 1536:1792] = (v * v).reshape(4, 2, 8, 256)
    x = dot(const("u2l"), g)
    v = yc[:, 256:384] + x[:64, :128] + x[64:, 128:]
    e1[:, :, :, 1792:1920] = (v * v).reshape(4, 2, 8, 128)
    for copy in far:
        copy.wait_recv()
    q = qr[0].astype(f32) + qr[1].astype(f32) + qr[2].astype(f32)
    v34 = kr[0] + kr[1] + (jr[0].astype(f32) + jr[1].astype(f32))[:72] + dot(const("x34"), rows(*split(q)))
    v = yc[:, 384:] + v34[:64]
    e1[:, :, :, 1920:] = (v * v).reshape(4, 2, 8, 128)
    pair1 = send(e1.at[:, 1 - core], ce1, partner)

    pair0e.wait_recv()
    over0e = along_y(e0e, ce0e, es0e, er0e)

    def taken(k, ref):
        for copy in gifts[k]:
            copy.wait_recv()
        a, b = ref[0], ref[1]
        z = [jnp.zeros((8, a.shape[1]), f32)] * (a.shape[0] == 4)
        hi, lo = split(rows(a, b, *z))
        return rows(hi, lo, hi)

    g = taken(0, gr0)
    q = dot(const("u0hi"), g)
    i0e[:, 0:1024] += q[:8]
    i0e[:, 1024:2048] += q[8:]
    i0e[:, 2048:] += dot(const("u0li"), g)
    g = taken(1, gr1)
    q = dot(const("u1hi"), g)
    i1[:, 0:512] += q[:8]
    i1[:, 512:1024] += q[8:]
    i1[:, 1024:] += dot(const("u1li"), g)
    g = taken(2, gr2)
    ic[:, 0:256] += dot(const("u2hi"), g)
    x = dot(const("u2li"), g)
    ic[:, 256:384] += x[:8, :128] + x[8:, 128:]
    ic[:, 384:] += v34[64:72]

    pair1.wait_recv()
    over1 = []
    for j in (2, 1, 3):
        q = lax.rem(ypos + j, 4)
        both = e1[q, core] + ce1[q]
        es2[j - 1] = both[:, 1536:]
        over1.append(send(es2.at[j - 1], er2.at[j - 1], at_y(j)))
        es1[j - 1] = fold(both[:, :1536])
        over1.append(send(es1.at[j - 1], er1.at[j - 1], at_y(j)))

    need(COUNT + 2)
    w = [weights[i] * (1.0 / (MEM - 1)) for i in range(16)]

    def scaled(energy, ref, k):
        third = ref.shape[1] // 3
        return [w[3 * k + j] * energy[:, third * n : third * n + third] * ref[:, third * n : third * n + third] for n, j in enumerate((0, 2, 1))]

    def keep(ref, values):
        third = ref.shape[1] // 3
        for n, v in enumerate(values):
            ref[:, third * n : third * n + third] = v

    keep(p0i, scaled(total(e0i, ce0i, er0i, over0i), i0i, 0))
    keep(p0e, scaled(total(e0e, ce0e, er0e, over0e), i0e, 0))
    ss0[0] = p0e[6:8]
    ss0[1] = p0e[0:2]
    syn0 = [send(ss0.at[n], sr0.at[n], at_tile(d)) for n, d in enumerate((1, -1))]

    v = e1[ypos, core] + ce1[ypos]
    for copy in over1:
        copy.wait_recv()
    energy = v[:, 1536:] + er2[0] + er2[1] + er2[2]
    row = lax.broadcasted_iota(jnp.int32, (8, 128), 0)
    lane = lax.broadcasted_iota(jnp.int32, (8, 128), 1)
    w34 = jnp.where(
        row < 2,
        jnp.where(row == 0, jnp.where(lane < 64, w[15], w[12]), jnp.where(lane < 64, w[13], w[14])),
        jnp.where(row < 4, w[9], jnp.where(row < 6, w[11], w[10])),
    )
    w2 = jnp.where(lax.broadcasted_iota(jnp.int32, (8, 256), 0) < 4, w[6], w[8])
    pc[:, 0:256] = w2 * energy[:, 0:256] * ic[:, 0:256]
    pc[:, 256:384] = w[7] * energy[:, 256:384] * ic[:, 256:384]
    pc[:, 384:] = w34 * energy[:, 384:] * ic[:, 384:]
    synt = [send(pc.at[:, 384:], srt.at[n], at_tile(d)) for n, d in enumerate((2, -2, 3, -3, -4))]
    sync = [send(pc, syc.at[n], at_tile(d)) for n, d in enumerate((1, -1))]
    energy = v[:, :1536] + unfold(er1[0]) + unfold(er1[1]) + unfold(er1[2])
    keep(p1, scaled(energy, i1, 1))
    ss1[0] = p1[4:8]
    ss1[1] = p1[0:4]
    syn1 = [send(ss1.at[n], sr1.at[n], at_tile(d)) for n, d in enumerate((1, -1))]

    bi = const("bi")
    bi_hi, bi_lo = bi[:768], bi[768:]

    def left(name, x):
        hi, lo = split(x)
        return dot(const(name), rows(hi, lo, hi))

    def columns(x):
        tall, half = x.shape[0], x.shape[1] // 2
        count = half // 128

        def win(j):
            return lanes(*[x[:, s + 128 * ((j + i) % count) : s + 128 * ((j + i) % count) + 128] for s in (0, half) for i in (-1, 0, 1)])

        a, b = split(rows(*[win(j) for j in range(count)]))
        r = dot(rows(a, b), bi_hi)
        r = r[: tall * count] + r[tall * count :] + dot(a, bi_lo)
        return lanes(*[r[tall * j : tall * j + tall] for j in range(count)])

    for copy in synt + sync:
        copy.wait_recv()
    t = {-2: srt[0], 2: srt[1], -3: srt[2], 3: srt[3], 4: srt[4], 0: pc[:, 384:], -1: syc[0, :, 384:], 1: syc[1, :, 384:]}
    stack = rows(*[t[b] for b in range(-3, 5)])
    hi, lo = split(left("s4", stack))
    m = const("i4")
    ll3 = dot(hi, m[:128]) + dot(lo, m[:128]) + dot(hi, m[128:])
    ll2 = columns(lanes(left("s3l", rows(stack, ll3, z8)), left("s3h", stack)))
    stack = rows(syc[0, :, 0:384], pc[:, 0:384], syc[1, :, 0:384], jnp.zeros((8, 384), f32))
    ll1 = columns(lanes(
        left("s2l0", rows(stack[:, 256:384], ll2[:, :128])),
        left("s2l1", rows(stack[:, 256:384], ll2[:, 128:])),
        left("s2h", stack[:, :256]),
    ))
    for copy in syn1:
        copy.wait_recv()
    stack = rows(p1[...], sr1[0], sr1[1])
    ll0 = columns(lanes(
        left("s1l", rows(ll1, stack[:, 1024:])),
        left("s1h", rows(stack[:, 0:512], stack[:, 512:1024])),
    ))
    for copy in syn0:
        copy.wait_recv()
    stack = rows(p0i[...], p0e[...], sr0[0], sr0[1], jnp.zeros((4, 3072), f32))
    out[...] = columns(lanes(
        left("s0l", rows(ll0, stack[:, 2048:])),
        left("s0h", rows(stack[:, 0:1024], stack[:, 1024:2048])),
    ))
    for copy in sent:
        copy.wait_send()


def local(members, increment, weights):
    arrays = packed()[0]
    anywhere = pl.BlockSpec(memory_space=pl.ANY)
    v = pltpu.VMEM
    scratch = [v(a.shape, bf16) for a in arrays] + [
        v((256, 2048), bf16), v((BAND, 2048), f32), pltpu.SMEM((16,), f32),
        v((288, 3968), bf16), v((288, 3968), bf16), v((128, 2048), bf16), v((128, 2048), bf16), v((32, 2048), bf16), v((32, 2048), bf16),
        v((8, 128), f32), v((64, 3072), f32), v((64, 1536), f32), v((64, 512), f32),
        v((8, 3072), f32), v((8, 3072), f32), v((8, 1536), f32), v((8, 512), f32),
        v((2, 32, 1024), bf16), v((2, 48, 512), bf16), v((2, 64, 256), bf16),
        v((2, 32, 1024), bf16), v((2, 48, 512), bf16), v((2, 64, 256), bf16),
        v((2, 4, 1024), f32), v((2, 8, 512), f32), v((2, 8, 256), f32),
        v((2, 4, 1024), f32), v((2, 8, 512), f32), v((2, 8, 256), f32),
        v((2, 72, 128), f32), v((2, 72, 128), f32), v((2, 80, 128), bf16), v((2, 80, 128), bf16), v((3, 32, 128), bf16), v((3, 32, 128), bf16),
        v((4, 2, 8, 3072), f32), v((4, 2, 8, 3072), f32), v((4, 2, 8, 2048), f32),
        v((4, 8, 3072), f32), v((4, 8, 3072), f32), v((4, 8, 2048), f32),
        v((3, 16, 1536), bf16), v((3, 16, 1536), bf16), v((3, 16, 768), bf16), v((3, 8, 512), f32),
        v((3, 16, 1536), bf16), v((3, 16, 1536), bf16), v((3, 16, 768), bf16), v((3, 8, 512), f32),
        v((8, 3072), f32), v((8, 3072), f32), v((8, 1536), f32), v((8, 512), f32),
        v((2, 2, 3072), f32), v((2, 4, 1536), f32), v((2, 2, 3072), f32), v((2, 4, 1536), f32),
        v((2, 8, 512), f32), v((5, 8, 128), f32),
        pltpu.SemaphoreType.DMA((48,)), pltpu.SemaphoreType.DMA((48,)), pltpu.SemaphoreType.DMA((COUNT + 3,)),
    ]
    result = pl.pallas_call(
        kernel,
        out_shape=jax.ShapeDtypeStruct((BAND, 2048), f32),
        in_specs=[anywhere] * (3 + COUNT),
        out_specs=pl.BlockSpec(memory_space=pltpu.VMEM),
        scratch_shapes=scratch,
        compiler_params=pltpu.CompilerParams(collective_id=0, has_side_effects=True, vmem_limit_bytes=56 * 2**20),
    )(members.reshape(256, 2048), increment.reshape(BAND, 2048), weights, *[jnp.asarray(a) for a in arrays])
    return result.reshape(1, BAND, 2048)


def solution(mesh):
    return jax.shard_map(
        local,
        mesh=mesh,
        in_specs=(P("mem", None, "tile", None), P("mem", "tile", None), P()),
        out_specs=P("mem", "tile", None),
        check_vma=False,
    )
```

```python
import functools

import jax
import jax.numpy as jnp
import numpy as np
from jax import lax
from jax.experimental import pallas as pl
from jax.experimental.pallas import tpu as pltpu
from jax.sharding import PartitionSpec as P

f32, bf16 = jnp.float32, jnp.bfloat16
MESH = pl.DeviceIdType.MESH
LIFT = (-1.586134342059924, -0.052980118572961, 0.882911075530934, 0.443506852043971)
KAPPA = 1.149604398860241
NROW, BAND, LEVELS, MEM, TILE = 1024, 32, 8, 8, 32
RANK = (2, 3, 4)


def forward_matrix(n):
    x = np.eye(n)
    e, o = x[0::2], x[1::2]
    after = lambda v: np.roll(v, -1, 0)
    before = lambda v: np.roll(v, 1, 0)
    o = o + LIFT[0] * (e + after(e))
    e = e + LIFT[1] * (before(o) + o)
    o = o + LIFT[2] * (e + after(e))
    e = e + LIFT[3] * (before(o) + o)
    return e * KAPPA, o / KAPPA


def inverse_matrix(n):
    z = np.eye(n)
    e, o = z[: n // 2] / KAPPA, z[n // 2 :] * KAPPA
    after = lambda v: np.roll(v, -1, 0)
    before = lambda v: np.roll(v, 1, 0)
    e = e - LIFT[3] * (before(o) + o)
    o = o - LIFT[2] * (e + after(e))
    e = e - LIFT[1] * (before(o) + o)
    o = o - LIFT[0] * (e + after(e))
    out = np.zeros((n, n))
    out[0::2], out[1::2] = e, o
    return out


def pieces(m):
    hi = np.asarray(m, np.float32).astype(bf16)
    lo = (np.asarray(m, np.float64) - hi.astype(np.float64)).astype(bf16)
    return hi, lo


def three(m):
    hi, lo = pieces(m)
    return np.concatenate([hi, hi, lo], axis=1)


def two(m):
    hi, lo = pieces(m)
    return np.concatenate([hi, lo], axis=1)


def per_field(m, fields, places=None):
    return np.kron(np.eye(fields), m)


def pad_rows(m, rows):
    return np.concatenate([m, np.zeros((rows - m.shape[0], m.shape[1]))], axis=0)


@functools.lru_cache(maxsize=None)
def constants():
    c = {}
    lows, highs, chain = [], [], np.eye(NROW)
    for k in range(5):
        low, high = forward_matrix(NROW >> k)
        lows.append(low @ chain)
        highs.append(high @ chain)
        chain = lows[-1]
    mid = 16

    def block(mat, k, d):
        r = (BAND >> k) // 2
        m = mat[mid * r : (mid + 1) * r, (mid - d) * BAND : (mid - d + 1) * BAND].copy()
        m[np.abs(m) < 1e-13] = 0.0
        return m

    def halves(m):
        return np.concatenate(pieces(m), axis=1)

    lo2048, hi2048 = forward_matrix(2048)
    bf = np.concatenate([lo2048[512:640, 896:1408], hi2048[512:640, 896:1408]], axis=0).T
    c["bf"] = np.concatenate(pieces(bf), axis=0)
    l256, h256 = forward_matrix(256)
    l128, h128 = forward_matrix(128)
    c["b34"] = np.concatenate(pieces(np.concatenate([l128 @ l256, h128 @ l256, h256, l256], axis=0).T), axis=0)
    s2048 = inverse_matrix(2048)
    bi = np.concatenate([s2048[1024:1280, 384:768], s2048[1024:1280, 1024 + 384 : 1024 + 768]], axis=1).T
    c["bi"] = np.concatenate(pieces(bi), axis=0)
    s256 = inverse_matrix(256).T
    c["i34"] = np.concatenate(pieces(np.concatenate([inverse_matrix(128).T @ s256[:128], s256], axis=0)), axis=0)

    inner, edge = list(range(4, 12)), [0, 1, 2, 3, 12, 13, 14, 15]
    for k in range(3):
        bl = {d: block(lows[k], k, d) for d in (0, 1, -1)}
        bh = {d: block(highs[k], k, d) for d in (0, 1, -1)}
        r = RANK[k]
        rows_h = 16 >> k
        place = {}
        for part in ("h", "l"):
            for d in (1, -1):
                full = np.concatenate([bl[d], bh[d]], axis=0) if part == "h" else bh[d]
                u, s, vt = np.linalg.svd(full, full_matrices=False)
                assert s[r:].max(initial=0.0) < 1e-12
                keep = s[:r] > 1e-12
                place[part, d] = (u[:, :r] * s[:r] * keep, vt[:r] * keep[:, None])
        top = lambda m: np.concatenate([m, 0 * m], axis=0)
        bot = lambda m: np.concatenate([0 * m, m], axis=0)
        for f, tag in ((8, "m"), (1, "i")):
            width = 8 * 2 * r if f == 8 else (4, 8, 8)[k]

            def sent(part):
                out = []
                for d in (1, -1):
                    v = place[part, d][1]
                    if f == 8:
                        out.append(per_field(v, f))
                    else:
                        out.append(pad_rows(np.concatenate([np.zeros((r if part == "l" else 0, BAND)), v], axis=0), 8))
                return out

            def spread(u, at):
                out = []
                for d in (1, -1):
                    m = np.zeros((u[d].shape[0], width))
                    m[:, at : at + u[d].shape[1]] = u[d]
                    out.append(m)
                m = np.concatenate(out, axis=1)
                if f == 1 and m.shape[1] < 16:
                    m = np.concatenate([m, np.zeros((m.shape[0], 16 - m.shape[1]))], axis=1)
                return m

            at_l = f * r
            if k == 0:
                own_h = [per_field(m[rows_], f) for rows_ in (inner, edge) for m in (bl[0], bh[0])]
                own_l = [per_field(bh[0][rows_], f) for rows_ in (inner, edge)]
                uh = {d: np.concatenate([per_field(place["h", d][0][:16][edge], f), per_field(place["h", d][0][16:][edge], f)], axis=0) for d in (1, -1)}
                ul = {d: per_field(place["l", d][0][edge], f) for d in (1, -1)}
                full_h = {d: place["h", d][0] for d in (1, -1)}
                assert all(np.abs(full_h[d][:16][inner]).max() < 1e-12 and np.abs(full_h[d][16:][inner]).max() < 1e-12 for d in full_h)
            elif k == 1:
                own_h = [per_field(bl[0], f), per_field(bh[0], f)]
                own_l = [per_field(bh[0], f)]
                uh = {d: np.concatenate([per_field(place["h", d][0][:rows_h], f), per_field(place["h", d][0][rows_h:], f)], axis=0) for d in (1, -1)}
                ul = {d: per_field(place["l", d][0], f) for d in (1, -1)}
            else:
                own_h = [per_field(np.concatenate([bl[0], bh[0]], axis=0), f)]
                own_l = [per_field(top(bh[0]), f), per_field(bot(bh[0]), f)]
                uh = {d: per_field(place["h", d][0], f) for d in (1, -1)}
                ul = {d: np.concatenate([per_field(top(place["l", d][0]), f), per_field(bot(place["l", d][0]), f)], axis=0) for d in (1, -1)}
            if k == 0 and f == 8:
                for part in ("h", "l"):
                    n, p = place[part, 1][1], place[part, -1][1]
                    assert np.abs(n[:, :24]).max() < 1e-12 and np.abs(p[:, 8:]).max() < 1e-12
                    n, p = per_field(n[:, 24:], f), per_field(p[:, :8], f)
                    z = np.zeros_like(n)
                    c[f"v0{part}"] = halves(np.concatenate([np.concatenate([n, z], axis=1), np.concatenate([z, p], axis=1)], axis=0))
                c["a0h"], c["a0l"] = halves(np.concatenate(own_h, axis=0)), halves(np.concatenate(own_l, axis=0))
            else:
                cut = halves if f == 8 else three
                c[f"a{k}h" + tag * (f == 1)] = cut(np.concatenate(own_h + sent("h"), axis=0))
                c[f"a{k}l" + tag * (f == 1)] = cut(np.concatenate(own_l + sent("l"), axis=0))
            cut = two if f == 8 else three
            c[f"u{k}h" + tag * (f == 1)] = cut(spread(uh, 0))
            c[f"u{k}l" + tag * (f == 1)] = cut(spread(ul, at_l))

    def tile34(d):
        z = np.zeros((8, 3 * BAND))
        z[0:1, :BAND], z[1:2, :BAND] = block(lows[4], 4, d), block(highs[4], 4, d)
        z[2:4, BAND : 2 * BAND] = block(lows[3], 3, d)
        z[4:6, BAND : 2 * BAND] = block(highs[3], 3, d)
        z[6:8, 2 * BAND :] = block(highs[3], 3, d)
        return z

    def tiles(z, f):
        return np.concatenate([per_field(z[:, i * BAND : (i + 1) * BAND], f) for i in range(3)], axis=1)

    for f, tag in ((8, "m"), (1, "i")):
        out = [tiles(tile34(d), f) for d in (0, 1, -1, 2, -2)]
        for d in (3, -3, 4):
            z = tile34(d)
            assert np.abs(z[2:]).max() == 0
            m = tiles(z[:2], f)
            out.append(m if f == 8 else pad_rows(m, 8))
        assert np.abs(tile34(-4)).max() == 0 and np.abs(tile34(5)).max() == 0 and np.abs(tile34(-5)).max() == 0
        m = np.concatenate(out, axis=0)
        c[f"w{tag}"] = halves(m) if f == 8 else three(m)
    spread = np.kron(np.eye(8), np.eye(8)[:, :2])
    c["x34"] = np.concatenate([spread, spread], axis=1).astype(bf16)

    def pick(k, start, stop, rows_out, low_slots, high_slots):
        n = NROW >> k
        m = inverse_matrix(n)
        m[np.abs(m) < 1e-13] = 0.0
        base = mid * (BAND >> k)
        part = m[base + start : base + stop]
        low, high = part[:, : n // 2], part[:, n // 2 :]
        half = base // 2
        out = np.zeros((rows_out, len(low_slots)))
        seen = 0.0
        for i in range(len(low_slots)):
            if low_slots[i] is not None:
                out[: stop - start, i] += low[:, half + low_slots[i]]
            if high_slots[i] is not None:
                out[: stop - start, i] += high[:, half + high_slots[i]]
        want = (np.abs(low).sum() if any(s is not None for s in low_slots) else 0.0) + (
            np.abs(high).sum() if any(s is not None for s in high_slots) else 0.0
        )
        assert abs(want - np.abs(out).sum()) < 1e-9, k
        return out


    none = [None]
    bands = list(range(-3, 5))
    flat = lambda rows: sum(rows, [])
    l4 = flat([[b] + none * 7 for b in bands])
    h4 = flat([none + [b] + none * 6 for b in bands])
    m4 = pick(4, -2, 6, 8, l4, h4)
    l3 = flat([none * 2 + [2 * b, 2 * b + 1] + none * 4 for b in bands])
    h3 = flat([none * 4 + [2 * b, 2 * b + 1] + none * 2 for b in bands])
    h3l = flat([none * 6 + [2 * b, 2 * b + 1] for b in bands])
    low3 = pick(3, -2, 8, 16, list(range(-2, 6)), none * 8)
    c["s34"] = three(np.concatenate([low3 @ m4, pick(3, -2, 8, 16, none * 64, h3l), pick(3, -2, 8, 16, l3, h3)], axis=0))
    near = (-1, 0, 1)
    l2 = flat([[4 * b + i for i in range(4)] + none * 4 for b in near]) + none * 8
    h2 = flat([none * 4 + [4 * b + i for i in range(4)] for b in near]) + none * 8
    c["s2h"] = three(pick(2, -2, 12, 16, l2, h2))
    low_ext = [-2 + i if i < 10 else None for i in range(16)]
    ha = flat([[4 * b + i for i in range(4)] + none * 4 for b in near]) + none * 8
    hb = flat([none * 4 + [4 * b + i for i in range(4)] for b in near]) + none * 8
    c["s2x"] = three(pick(2, -2, 12, 16, low_ext, none * 16))
    c["s2p"] = three(np.concatenate([pick(2, -2, 12, 16, none * 32, ha), pick(2, -2, 12, 16, none * 32, hb)], axis=0))
    s1 = list(range(8)) + list(range(-4, 0)) + list(range(8, 12))
    c["s1h"] = three(pick(1, -2, 18, 24, s1 + none * 16, none * 16 + s1))
    low_ext = [-2 + i if i < 14 else None for i in range(16)]
    c["s1x"] = three(pick(1, -2, 18, 24, low_ext, none * 16))
    c["s1p"] = three(pick(1, -2, 18, 24, none * 16, s1))
    s0 = inner + edge + [-2, -1, 16, 17] + none * 12
    c["s0h"] = three(pick(0, 0, 32, 32, s0 + none * 32, none * 32 + s0))
    low_ext = [-2 + i if i < 20 else None for i in range(32)]
    c["s0x"] = three(pick(0, 0, 32, 32, low_ext, none * 32))
    c["s0p"] = three(pick(0, 0, 32, 32, none * 32, s0))
    return c


GROUPS = (
    ("bf",),
    ("v0h", "v0l", "b34", "a1h", "a1l", "a2h", "a2l"),
    ("wm",),
    ("a0h", "a0l"),
    ("a0hi", "a0li", "a1hi", "a1li", "a2hi", "a2li", "wi"),
    ("u0h", "u0l", "u1h", "u1l", "u2h", "u2l", "x34", "u0hi", "u0li", "u1hi", "u1li", "u2hi", "u2li"),
    ("i34", "s34", "s2h", "s2x", "s2p", "s1h", "s1x", "s1p", "s0h", "s0x", "s0p"),
    ("bi",),
)


@functools.lru_cache(maxsize=None)
def packed():
    c = constants()
    assert sorted(sum(GROUPS, ())) == sorted(c)
    arrays, where = [], {}
    for g, names in enumerate(GROUPS):
        wide = max(-(-c[n].shape[1] // 128) * 128 for n in names)
        parts, at = [], 0
        for n in names:
            m = c[n]
            tall = -(-m.shape[0] // 16) * 16
            full = np.zeros((tall, wide), bf16)
            full[: m.shape[0], : m.shape[1]] = m
            parts.append(full)
            where[n] = (g, at, m.shape[0], m.shape[1])
            at += tall
        arrays.append(np.concatenate(parts, axis=0))
    return arrays, where


def split(x):
    hi = x.astype(bf16)
    return hi, (x - hi.astype(f32)).astype(bf16)


def dot(a, b):
    return jnp.dot(a, b, preferred_element_type=f32)


def rows(*parts):
    return jnp.concatenate(parts, axis=0)


def lanes(*parts):
    return jnp.concatenate(parts, axis=1) if len(parts) > 1 else parts[0]


COUNT = len(GROUPS)
NEXT, FAR = (1, -1), (2, -2, 3, -3, -4)


def kernel(members_hbm, increment_hbm, weights_hbm, *refs):
    groups_hbm, out, groups = refs[:COUNT], refs[COUNT], refs[COUNT + 1 : 2 * COUNT + 1]
    (members, increment, weights, t_hi, t_lo, b_hi, b_lo, u_hi, u_lo,
     y0e, y1, yc, i0i, i0e, i1, ic,
     hs0, hs1, hs2, hr0, hr1, hr2, gs0, gs1, gs2, gr0, gr1, gr2,
     ks, kr, js, jr, qs, qr, gks, gkr,
     e0i, e0e, e1, ec, ce0i, ce0e, ce1, cec, es0i, es0e, es1, es2, er0i, er0e, er1, er2,
     syc, srt, p0i, p0e, p1, pc, ss0, ss1, sr0, sr1,
     sem_s, sem_r, sem_l) = refs[2 * COUNT + 1 :]
    where = packed()[1]
    mem, tile = lax.axis_index("mem"), lax.axis_index("tile")
    ypos, core = lax.div(mem, 2), lax.rem(mem, 2)

    def at_tile(d):
        return (mem, lax.rem(tile + TILE + d, TILE))

    def at_y(j):
        return (lax.rem(ypos + j, 4) * 2 + core, tile)

    partner = (ypos * 2 + 1 - core, tile)
    near = [at_tile(d) for d in (1, -1, 2, -2, 3, -3, 4, -4)] + [partner] + [at_y(j) for j in (1, 2, 3)]
    barrier = pltpu.get_barrier_semaphore()
    for device in near:
        pl.semaphore_signal(barrier, inc=1, device_id=device, device_id_type=MESH)

    sources = [(groups_hbm[0], groups[0]), (members_hbm, members), (increment_hbm, increment)]
    sources += [(groups_hbm[g], groups[g]) for g in range(1, COUNT)] + [(weights_hbm, weights)]
    loads = [pltpu.make_async_copy(a, b, sem_l.at[n]) for n, (a, b) in enumerate(sources)]
    order = [0] + list(range(3, COUNT + 2))
    begun, loaded = set(), set()

    def begin(*which):
        for n in which:
            loads[n].start()
            begun.add(n)

    def need(n):
        if n not in loaded:
            loads[n].wait()
            loaded.add(n)

    def const(name):
        g, at, tall, wide = where[name]
        need(order[g])
        return groups[g][at : at + tall, :wide]

    def triple(name):
        m = const(name)
        half = m.shape[1] // 2
        return lanes(m[:, :half], m[:, :half], m[:, half:])

    sent = []

    def send(src, dst, device):
        n = len(sent)
        if n == 0:
            pl.semaphore_wait(barrier, len(near))
        copy = pltpu.make_async_remote_copy(
            src_ref=src, dst_ref=dst, send_sem=sem_s.at[n], recv_sem=sem_r.at[n], device_id=device, device_id_type=MESH
        )
        copy.start()
        sent.append(copy)
        return copy

    def window(ref, width, j, first, last):
        start = 256 * j - 128
        groups_ = []
        for t in [(start // 128 + i) % (width // 128) for i in range(4)]:
            if groups_ and groups_[-1][1] == t:
                groups_[-1][1] = t + 1
            else:
                groups_.append([t, t + 1])
        return lanes(*[ref[first:last, 128 * a : 128 * b] for a, b in groups_])

    def put(hi_ref, lo_ref, first, last, width, j, r):
        half = width // 2
        for ref, v in zip((hi_ref, lo_ref), split(r)):
            ref[first:last, 128 * j : 128 * j + 128] = v[:, :128]
            ref[first:last, half + 128 * j : half + 128 * j + 128] = v[:, 128:]

    base = [0, 2048, 3072]
    begin(0, 1)
    bf = const("bf")
    bf_hi, bf_lo = bf[:512], bf[512:]
    need(1)
    begin(3, 4, 2, 5, 6, 7)
    for j in range(8):
        w = window(members, 2048, j, 0, 256)
        r = dot(w, bf_hi) + dot(w, bf_lo)
        put(t_hi, t_lo, 0, 256, 2048, j, r)
        r = r.reshape(8, 32, 256)
        put(b_hi, b_lo, 0, 128, 2048, j, rows(r[:, 24:].reshape(64, 256), r[:, :8].reshape(64, 256)))

    def part(k, which, first, last):
        half = 1024 >> k
        s = base[k] + (half if which == "h" else 0)
        hi, lo = t_hi[first:last, s : s + half], t_lo[first:last, s : s + half]
        return rows(hi, lo, hi)

    owed = {}
    for which, s in (("h", 1024), ("l", 0)):
        hi, lo = b_hi[:, s : s + 1024], b_lo[:, s : s + 1024]
        owed[which] = dot(triple("v0" + which), rows(hi, lo, hi))
    halos = [[], [], []]

    def share(k, h, l, hs, hr):
        half = h.shape[0] // 2
        for n, d in enumerate((1, -1)):
            hs[n] = rows(h[n * half : n * half + half], l[n * half : n * half + half]).astype(bf16)
            halos[k].append(send(hs.at[n], hr.at[n], at_tile(d)))

    share(0, owed["h"], owed["l"], hs0, hr0)

    def down(k, first, last):
        width, s = 2048 >> k, base[k - 1]
        tall, count = last - first, width // 256
        each = 1 if tall > 32 else count
        for j in range(0, count, each):
            a = rows(*[window(t_hi.at[:, s : s + width], width, i, first, last) for i in range(j, j + each)])
            b = rows(*[window(t_lo.at[:, s : s + width], width, i, first, last) for i in range(j, j + each)])
            r = dot(a, bf_hi) + dot(b, bf_hi) + dot(a, bf_lo)
            for i in range(each):
                put(t_hi.at[:, base[k] : base[k] + width], t_lo.at[:, base[k] : base[k] + width], first, last, width, j + i, r[tall * i : tall * i + tall])

    begin(*range(8, COUNT + 3))
    down(1, 0, 256)
    share(1, dot(triple("a1h")[128:], part(1, "h", 0, 256)), dot(triple("a1l")[64:], part(1, "l", 0, 256)), hs1, hr1)
    down(2, 0, 256)
    share(2, dot(triple("a2h")[64:], part(2, "h", 0, 256)), dot(triple("a2l")[128:], part(2, "l", 0, 256)), hs2, hr2)

    def stack34(first, last):
        m, s = const("b34"), base[2]
        a, b = t_hi[first:last, s : s + 256], t_lo[first:last, s : s + 256]
        r = dot(a, m[:256]) + dot(b, m[:256]) + dot(a, m[256:])
        hi, lo = split(rows(r[:, :128], r[:, 128:256], r[:, 256:]))
        return rows(hi, lo, hi)

    wm = dot(triple("wm"), stack34(0, 256))
    yc[:, 384:] = wm[0:64]
    far = []
    for n, d in enumerate((1, -1)):
        ks[n] = wm[64 + 64 * n : 128 + 64 * n]
        far.append(send(ks.at[n], kr.at[n], at_tile(d)))
    for n, d in enumerate((2, -2)):
        js[n] = wm[192 + 64 * n : 256 + 64 * n].astype(bf16)
        far.append(send(js.at[n], jr.at[n], at_tile(d)))
    for n, d in enumerate((3, -3, 4)):
        qs[n] = wm[320 + 16 * n : 336 + 16 * n].astype(bf16)
        far.append(send(qs.at[n], qr.at[n], at_tile(d)))

    y = dot(triple("a0h"), part(0, "h", 0, 256))
    x = dot(triple("a0l"), part(0, "l", 0, 256))
    for n, v in enumerate((y[:64], y[64:128], x[:64])):
        e0i[:, :, :, 1024 * n : 1024 * n + 1024] = (v * v).reshape(4, 2, 8, 1024)
    pair0i = send(e0i.at[:, 1 - core], ce0i, partner)
    y0e[:, 0:1024], y0e[:, 1024:2048], y0e[:, 2048:] = y[128:192], y[192:], x[64:]

    h = dot(triple("a1h")[:128], part(1, "h", 0, 256))
    l = dot(triple("a1l")[:64], part(1, "l", 0, 256))
    y1[:, 0:512], y1[:, 512:1024], y1[:, 1024:] = h[:64], h[64:], l
    h = dot(triple("a2h")[:64], part(2, "h", 0, 256))
    l = dot(triple("a2l")[:128], part(2, "l", 0, 256))
    yc[:, 0:256], yc[:, 256:384] = h, l[:64, :128] + l[64:, 128:]

    need(2)
    hi, lo = split(increment[...])
    u_hi[...], u_lo[...] = hi, lo
    a = rows(*[window(u_hi, 2048, j, 0, 32) for j in range(8)])
    b = rows(*[window(u_lo, 2048, j, 0, 32) for j in range(8)])
    r = dot(rows(a, b), bf_hi)
    r = r[:256] + r[256:] + dot(a, bf_lo)
    for j in range(8):
        put(t_hi, t_lo, 256, 288, 2048, j, r[32 * j : 32 * j + 32])
    for k in (1, 2):
        down(k, 256, 288)
    gifts = [[], [], []]

    def give(k, n8, p8, gs, gr):
        tall = gs.shape[1]
        for n, (d, v) in enumerate(((1, n8), (-1, p8))):
            gs[n] = v[:tall]
            gifts[k].append(send(gs.at[n], gr.at[n], at_tile(d)))

    y = dot(const("a0hi"), part(0, "h", 256, 288))
    x = dot(const("a0li"), part(0, "l", 256, 288))
    give(0, y[32:40] + x[16:24], y[40:48] + x[24:32], gs0, gr0)
    i0i[:, 0:1024], i0i[:, 1024:2048], i0i[:, 2048:] = y[:8], y[8:16], x[:8]
    i0e[:, 0:1024], i0e[:, 1024:2048], i0e[:, 2048:] = y[16:24], y[24:32], x[8:16]
    y = dot(const("a1hi"), part(1, "h", 256, 288))
    x = dot(const("a1li"), part(1, "l", 256, 288))
    give(1, y[16:24] + x[8:16], y[24:32] + x[16:24], gs1, gr1)
    i1[:, 0:512], i1[:, 512:1024], i1[:, 1024:] = y[:8], y[8:16], x[:8]
    y = dot(const("a2hi"), part(2, "h", 256, 288))
    x = dot(const("a2li"), part(2, "l", 256, 288))
    give(2, y[8:16] + x[16:24], y[16:24] + x[24:32], gs2, gr2)
    ic[:, 0:256], ic[:, 256:384] = y[:8], x[:8, :128] + x[8:16, 128:]

    wi = dot(const("wi"), stack34(256, 288))
    ic[:, 384:] = wi[0:8]
    z8 = jnp.zeros((8, 128), f32)
    farther = []
    for n, d in enumerate((1, -1, 2, -2, 3, -3, 4)):
        gks[n] = wi[8 + 8 * n : 16 + 8 * n]
        farther.append(send(gks.at[n], gkr.at[n], at_tile(d)))

    def fold(v):
        half = v.shape[1] // 2
        v = v * v
        return rows(v[:, :half], v[:, half:]).astype(bf16)

    def unfold(v):
        v = jnp.sqrt(v.astype(f32))
        return lanes(v[:8], v[8:])

    def along_y(e, ce, es, er):
        copies = []
        for j in (2, 1, 3):
            q = lax.rem(ypos + j, 4)
            es[j - 1] = fold(e[q, core] + ce[q])
            copies.append(send(es.at[j - 1], er.at[j - 1], at_y(j)))
        return copies

    def total(e, ce, er, copies):
        v = e[ypos, core] + ce[ypos]
        for copy in copies:
            copy.wait_recv()
        return v + unfold(er[0]) + unfold(er[1]) + unfold(er[2])

    pair0i.wait_recv()
    over0i = along_y(e0i, ce0i, es0i, er0i)

    def got(k, ref):
        for copy in halos[k]:
            copy.wait_recv()
        a, b = ref[0], ref[1]
        return rows(a, b, a, b)

    g = got(0, hr0)
    q = dot(const("u0h"), g)
    x = dot(const("u0l"), g)
    for n, v in enumerate((q[:64], q[64:], x)):
        v = v + y0e[:, 1024 * n : 1024 * n + 1024]
        e0e[:, :, :, 1024 * n : 1024 * n + 1024] = (v * v).reshape(4, 2, 8, 1024)
    pair0e = send(e0e.at[:, 1 - core], ce0e, partner)

    g = got(1, hr1)
    q = dot(const("u1h"), g)
    x = dot(const("u1l"), g)
    for n, v in enumerate((q[:64], q[64:], x)):
        v = v + y1[:, 512 * n : 512 * n + 512]
        e1[:, :, :, 512 * n : 512 * n + 512] = (v * v).reshape(4, 2, 8, 512)
    pair1 = send(e1.at[:, 1 - core], ce1, partner)

    g = got(2, hr2)
    v = yc[:, 0:256] + dot(const("u2h"), g)
    ec[:, :, :, 0:256] = (v * v).reshape(4, 2, 8, 256)
    x = dot(const("u2l"), g)
    v = yc[:, 256:384] + x[:64, :128] + x[64:, 128:]
    ec[:, :, :, 256:384] = (v * v).reshape(4, 2, 8, 128)
    pair0e.wait_recv()
    over0e = along_y(e0e, ce0e, es0e, er0e)
    pair1.wait_recv()
    over1 = along_y(e1, ce1, es1, er1)
    for copy in far:
        copy.wait_recv()
    q = qr[0].astype(f32) + qr[1].astype(f32) + qr[2].astype(f32)
    v34 = kr[0] + kr[1] + jr[0].astype(f32) + jr[1].astype(f32) + dot(const("x34"), rows(*split(q)))
    v = yc[:, 384:] + v34
    ec[:, :, :, 384:] = (v * v).reshape(4, 2, 8, 128)
    pairc = send(ec.at[:, 1 - core], cec, partner)
    def taken(k, ref):
        for copy in gifts[k]:
            copy.wait_recv()
        a, b = ref[0], ref[1]
        z = [jnp.zeros((8, a.shape[1]), f32)] * (a.shape[0] == 4)
        hi, lo = split(rows(a, b, *z))
        return rows(hi, lo, hi)

    g = taken(0, gr0)
    q = dot(const("u0hi"), g)
    i0e[:, 0:1024] += q[:8]
    i0e[:, 1024:2048] += q[8:]
    i0e[:, 2048:] += dot(const("u0li"), g)
    g = taken(1, gr1)
    q = dot(const("u1hi"), g)
    i1[:, 0:512] += q[:8]
    i1[:, 512:1024] += q[8:]
    i1[:, 1024:] += dot(const("u1li"), g)
    g = taken(2, gr2)
    ic[:, 0:256] += dot(const("u2hi"), g)
    x = dot(const("u2li"), g)
    ic[:, 256:384] += x[:8, :128] + x[8:, 128:]
    for copy in farther:
        copy.wait_recv()
    v = gkr[0] + gkr[1] + gkr[2] + gkr[3]
    row = lax.broadcasted_iota(jnp.int32, (8, 128), 0)
    ic[:, 384:] += v + jnp.where(row < 2, gkr[4] + gkr[5] + gkr[6], 0.0)
    pairc.wait_recv()
    overc = []
    for j in (2, 1, 3):
        q = lax.rem(ypos + j, 4)
        es2[j - 1] = ec[q, core] + cec[q]
        overc.append(send(es2.at[j - 1], er2.at[j - 1], at_y(j)))

    need(COUNT + 2)
    w = [weights[i] * (1.0 / (MEM - 1)) for i in range(16)]

    def scaled(energy, ref, k):
        third = ref.shape[1] // 3
        return [w[3 * k + j] * energy[:, third * n : third * n + third] * ref[:, third * n : third * n + third] for n, j in enumerate((0, 2, 1))]

    def keep(ref, values):
        third = ref.shape[1] // 3
        for n, v in enumerate(values):
            ref[:, third * n : third * n + third] = v

    keep(p0i, scaled(total(e0i, ce0i, er0i, over0i), i0i, 0))
    keep(p0e, scaled(total(e0e, ce0e, er0e, over0e), i0e, 0))
    ss0[0] = p0e[6:8]
    ss0[1] = p0e[0:2]
    syn0 = [send(ss0.at[n], sr0.at[n], at_tile(d)) for n, d in enumerate((1, -1))]

    keep(p1, scaled(total(e1, ce1, er1, over1), i1, 1))
    ss1[0] = p1[4:8]
    ss1[1] = p1[0:4]
    syn1 = [send(ss1.at[n], sr1.at[n], at_tile(d)) for n, d in enumerate(NEXT)]

    lane = lax.broadcasted_iota(jnp.int32, (8, 128), 1)
    w34 = jnp.where(
        row < 2,
        jnp.where(row == 0, jnp.where(lane < 64, w[15], w[12]), jnp.where(lane < 64, w[13], w[14])),
        jnp.where(row < 4, w[9], jnp.where(row < 6, w[11], w[10])),
    )
    w2 = jnp.where(lax.broadcasted_iota(jnp.int32, (8, 256), 0) < 4, w[6], w[8])
    v = ec[ypos, core] + cec[ypos]
    for copy in overc:
        copy.wait_recv()
    pc[...] = lanes(w2, jnp.full((8, 128), w[7]), w34) * (v + er2[0] + er2[1] + er2[2]) * ic[...]
    sync = [send(pc.at[:, 384:], srt.at[n], at_tile(d)) for n, d in enumerate(FAR)]
    sync += [send(pc, syc.at[n], at_tile(d)) for n, d in enumerate(NEXT)]

    bi = const("bi")
    bi_hi, bi_lo = bi[:768], bi[768:]

    def left(name, x):
        hi, lo = split(x)
        return dot(const(name), rows(hi, lo, hi))

    def columns(x, sides=2):
        tall, half = x.shape[0], x.shape[1] // sides
        count = half // 128
        starts = (0, half)[:sides]

        def win(j):
            return lanes(*[x[:, s + 128 * ((j + i) % count) : s + 128 * ((j + i) % count) + 128] for s in starts for i in (-1, 0, 1)])

        a, b = split(rows(*[win(j) for j in range(count)]))
        r = dot(rows(a, b), bi_hi[: 384 * sides])
        r = r[: tall * count] + r[tall * count :] + dot(a, bi_lo[: 384 * sides])
        return lanes(*[r[tall * j : tall * j + tall] for j in range(count)])

    for copy in syn0:
        copy.wait_recv()
    stack = rows(p0i[...], p0e[...], sr0[0], sr0[1], jnp.zeros((12, 3072), f32))
    out[...] = columns(lanes(left("s0p", stack[:, 2048:]), left("s0h", rows(stack[:, 0:1024], stack[:, 1024:2048]))))
    for copy in syn1:
        copy.wait_recv()
    stack = rows(p1[...], sr1[0], sr1[1])
    base0 = columns(lanes(left("s1p", stack[:, 1024:]), left("s1h", rows(stack[:, 0:512], stack[:, 512:1024]))))

    for copy in sync:
        copy.wait_recv()
    own, beside = pc[...], [syc[0], syc[1]]
    t = {0: own[:, 384:], -1: beside[0][:, 384:], 1: beside[1][:, 384:]}
    for n, d in enumerate(FAR):
        t[-d] = srt[n]
    x = left("s34", rows(*[t[b] for b in range(-3, 5)]))
    hi, lo = split(lanes(x[:16], x[16:32], x[32:]))
    m = const("i34")
    ll2 = dot(hi, m[:384]) + dot(lo, m[:384]) + dot(hi, m[384:])
    stack = rows(beside[0][:, 0:384], own[:, 0:384], beside[1][:, 0:384], jnp.zeros((8, 384), f32))
    x = left("s2p", stack[:, 256:])
    base1 = columns(lanes(x[:16], x[16:], left("s2h", stack[:, :256])))
    ll1 = base1 + columns(left("s2x", ll2), 1)
    ll0 = base0 + columns(left("s1x", ll1), 1)
    out[...] += columns(left("s0x", rows(ll0, jnp.zeros((8, 1024), f32))), 1)
    for copy in sent:
        copy.wait_send()


def local(members, increment, weights):
    arrays = packed()[0]
    anywhere = pl.BlockSpec(memory_space=pl.ANY)
    v = pltpu.VMEM
    scratch = [v(a.shape, bf16) for a in arrays] + [
        v((256, 2048), bf16), v((BAND, 2048), f32), pltpu.SMEM((16,), f32),
        v((288, 3584), bf16), v((288, 3584), bf16), v((128, 2048), bf16), v((128, 2048), bf16), v((32, 2048), bf16), v((32, 2048), bf16),
        v((64, 3072), f32), v((64, 1536), f32), v((64, 512), f32),
        v((8, 3072), f32), v((8, 3072), f32), v((8, 1536), f32), v((8, 512), f32),
        v((2, 32, 1024), bf16), v((2, 48, 512), bf16), v((2, 64, 256), bf16),
        v((2, 32, 1024), bf16), v((2, 48, 512), bf16), v((2, 64, 256), bf16),
        v((2, 4, 1024), f32), v((2, 8, 512), f32), v((2, 8, 256), f32),
        v((2, 4, 1024), f32), v((2, 8, 512), f32), v((2, 8, 256), f32),
        v((2, 64, 128), f32), v((2, 64, 128), f32), v((2, 64, 128), bf16), v((2, 64, 128), bf16), v((3, 16, 128), bf16), v((3, 16, 128), bf16),
        v((7, 8, 128), f32), v((7, 8, 128), f32),
        v((4, 2, 8, 3072), f32), v((4, 2, 8, 3072), f32), v((4, 2, 8, 1536), f32), v((4, 2, 8, 512), f32),
        v((4, 8, 3072), f32), v((4, 8, 3072), f32), v((4, 8, 1536), f32), v((4, 8, 512), f32),
        v((3, 16, 1536), bf16), v((3, 16, 1536), bf16), v((3, 16, 768), bf16), v((3, 8, 512), f32),
        v((3, 16, 1536), bf16), v((3, 16, 1536), bf16), v((3, 16, 768), bf16), v((3, 8, 512), f32),
        v((2, 8, 512), f32), v((5, 8, 128), f32),
        v((8, 3072), f32), v((8, 3072), f32), v((8, 1536), f32), v((8, 512), f32),
        v((2, 2, 3072), f32), v((2, 4, 1536), f32), v((2, 2, 3072), f32), v((2, 4, 1536), f32),
        pltpu.SemaphoreType.DMA((96,)), pltpu.SemaphoreType.DMA((96,)), pltpu.SemaphoreType.DMA((COUNT + 3,)),
    ]
    result = pl.pallas_call(
        kernel,
        out_shape=pltpu.VMEM((BAND, 2048), f32),
        in_specs=[anywhere] * (3 + COUNT),
        out_specs=pl.BlockSpec(memory_space=pltpu.VMEM),
        scratch_shapes=scratch,
        compiler_params=pltpu.CompilerParams(collective_id=0, has_side_effects=True, vmem_limit_bytes=56 * 2**20),
    )(members.reshape(256, 2048), increment.reshape(BAND, 2048), weights, *[jnp.asarray(a) for a in arrays])
    return result.reshape(1, BAND, 2048)


def solution(mesh):
    return jax.shard_map(
        local,
        mesh=mesh,
        in_specs=(P("mem", None, "tile", None), P("mem", "tile", None), P()),
        out_specs=P("mem", "tile", None),
        check_vma=False,
    )
```

```python
import functools

import jax
import jax.numpy as jnp
import numpy as np
from jax import lax
from jax.experimental import pallas as pl
from jax.experimental.pallas import tpu as pltpu
from jax.sharding import PartitionSpec as P

f32, bf16 = jnp.float32, jnp.bfloat16
MESH = pl.DeviceIdType.MESH
LIFT = (-1.586134342059924, -0.052980118572961, 0.882911075530934, 0.443506852043971)
KAPPA = 1.149604398860241
NROW, BAND, LEVELS, MEM, TILE = 1024, 32, 8, 8, 32
RANK = (2, 3, 4)


def forward_matrix(n):
    x = np.eye(n)
    e, o = x[0::2], x[1::2]
    after = lambda v: np.roll(v, -1, 0)
    before = lambda v: np.roll(v, 1, 0)
    o = o + LIFT[0] * (e + after(e))
    e = e + LIFT[1] * (before(o) + o)
    o = o + LIFT[2] * (e + after(e))
    e = e + LIFT[3] * (before(o) + o)
    return e * KAPPA, o / KAPPA


def inverse_matrix(n):
    z = np.eye(n)
    e, o = z[: n // 2] / KAPPA, z[n // 2 :] * KAPPA
    after = lambda v: np.roll(v, -1, 0)
    before = lambda v: np.roll(v, 1, 0)
    e = e - LIFT[3] * (before(o) + o)
    o = o - LIFT[2] * (e + after(e))
    e = e - LIFT[1] * (before(o) + o)
    o = o - LIFT[0] * (e + after(e))
    out = np.zeros((n, n))
    out[0::2], out[1::2] = e, o
    return out


def pieces(m):
    hi = np.asarray(m, np.float32).astype(bf16)
    lo = (np.asarray(m, np.float64) - hi.astype(np.float64)).astype(bf16)
    return hi, lo


def three(m):
    hi, lo = pieces(m)
    return np.concatenate([hi, hi, lo], axis=1)


def two(m):
    hi, lo = pieces(m)
    return np.concatenate([hi, lo], axis=1)


def per_field(m, fields, places=None):
    return np.kron(np.eye(fields), m)


def pad_rows(m, rows):
    return np.concatenate([m, np.zeros((rows - m.shape[0], m.shape[1]))], axis=0)


@functools.lru_cache(maxsize=None)
def constants():
    c = {}
    lows, highs, chain = [], [], np.eye(NROW)
    for k in range(5):
        low, high = forward_matrix(NROW >> k)
        lows.append(low @ chain)
        highs.append(high @ chain)
        chain = lows[-1]
    mid = 16

    def block(mat, k, d):
        r = (BAND >> k) // 2
        m = mat[mid * r : (mid + 1) * r, (mid - d) * BAND : (mid - d + 1) * BAND].copy()
        m[np.abs(m) < 1e-13] = 0.0
        return m

    def halves(m):
        return np.concatenate(pieces(m), axis=1)

    lo2048, hi2048 = forward_matrix(2048)
    bf = np.concatenate([lo2048[512:640, 896:1408], hi2048[512:640, 896:1408]], axis=0).T
    c["bf"] = np.concatenate(pieces(bf), axis=0)
    l256, h256 = forward_matrix(256)
    l128, h128 = forward_matrix(128)
    c["b34"] = np.concatenate(pieces(np.concatenate([l128 @ l256, h128 @ l256, h256, l256], axis=0).T), axis=0)
    s2048 = inverse_matrix(2048)
    bi = np.concatenate([s2048[1024:1280, 384:768], s2048[1024:1280, 1024 + 384 : 1024 + 768]], axis=1).T
    c["bi"] = np.concatenate(pieces(bi), axis=0)
    s256 = inverse_matrix(256).T
    c["i34"] = np.concatenate(pieces(np.concatenate([inverse_matrix(128).T @ s256[:128], s256], axis=0)), axis=0)

    inner, edge = list(range(4, 12)), [0, 1, 2, 3, 12, 13, 14, 15]
    for k in range(3):
        bl = {d: block(lows[k], k, d) for d in (0, 1, -1)}
        bh = {d: block(highs[k], k, d) for d in (0, 1, -1)}
        r = RANK[k]
        rows_h = 16 >> k
        place = {}
        for part in ("h", "l"):
            for d in (1, -1):
                full = np.concatenate([bl[d], bh[d]], axis=0) if part == "h" else bh[d]
                u, s, vt = np.linalg.svd(full, full_matrices=False)
                assert s[r:].max(initial=0.0) < 1e-12
                keep = s[:r] > 1e-12
                place[part, d] = (u[:, :r] * s[:r] * keep, vt[:r] * keep[:, None])
        top = lambda m: np.concatenate([m, 0 * m], axis=0)
        bot = lambda m: np.concatenate([0 * m, m], axis=0)
        for f, tag in ((8, "m"), (1, "i")):
            width = 8 * 2 * r if f == 8 else (4, 8, 8)[k]

            def sent(part):
                out = []
                for d in (1, -1):
                    v = place[part, d][1]
                    if f == 8:
                        out.append(per_field(v, f))
                    else:
                        out.append(pad_rows(np.concatenate([np.zeros((r if part == "l" else 0, BAND)), v], axis=0), 8))
                return out

            def spread(u, at):
                out = []
                for d in (1, -1):
                    m = np.zeros((u[d].shape[0], width))
                    m[:, at : at + u[d].shape[1]] = u[d]
                    out.append(m)
                m = np.concatenate(out, axis=1)
                if f == 1 and m.shape[1] < 16:
                    m = np.concatenate([m, np.zeros((m.shape[0], 16 - m.shape[1]))], axis=1)
                return m

            at_l = f * r
            if k == 0:
                own_h = [per_field(m[rows_], f) for rows_ in (inner, edge) for m in (bl[0], bh[0])]
                own_l = [per_field(bh[0][rows_], f) for rows_ in (inner, edge)]
                uh = {d: np.concatenate([per_field(place["h", d][0][:16][edge], f), per_field(place["h", d][0][16:][edge], f)], axis=0) for d in (1, -1)}
                ul = {d: per_field(place["l", d][0][edge], f) for d in (1, -1)}
                full_h = {d: place["h", d][0] for d in (1, -1)}
                assert all(np.abs(full_h[d][:16][inner]).max() < 1e-12 and np.abs(full_h[d][16:][inner]).max() < 1e-12 for d in full_h)
            elif k == 1:
                own_h = [per_field(bl[0], f), per_field(bh[0], f)]
                own_l = [per_field(bh[0], f)]
                uh = {d: np.concatenate([per_field(place["h", d][0][:rows_h], f), per_field(place["h", d][0][rows_h:], f)], axis=0) for d in (1, -1)}
                ul = {d: per_field(place["l", d][0], f) for d in (1, -1)}
            else:
                own_h = [per_field(np.concatenate([bl[0], bh[0]], axis=0), f)]
                own_l = [per_field(top(bh[0]), f), per_field(bot(bh[0]), f)]
                uh = {d: per_field(place["h", d][0], f) for d in (1, -1)}
                ul = {d: np.concatenate([per_field(top(place["l", d][0]), f), per_field(bot(place["l", d][0]), f)], axis=0) for d in (1, -1)}
            if k == 0 and f == 8:
                for part in ("h", "l"):
                    n, p = place[part, 1][1], place[part, -1][1]
                    assert np.abs(n[:, :24]).max() < 1e-12 and np.abs(p[:, 8:]).max() < 1e-12
                    n, p = per_field(n[:, 24:], f), per_field(p[:, :8], f)
                    z = np.zeros_like(n)
                    c[f"v0{part}"] = halves(np.concatenate([np.concatenate([n, z], axis=1), np.concatenate([z, p], axis=1)], axis=0))
                c["a0h"], c["a0l"] = halves(np.concatenate(own_h, axis=0)), halves(np.concatenate(own_l, axis=0))
            else:
                cut = halves if f == 8 else three
                c[f"a{k}h" + tag * (f == 1)] = cut(np.concatenate(own_h + sent("h"), axis=0))
                c[f"a{k}l" + tag * (f == 1)] = cut(np.concatenate(own_l + sent("l"), axis=0))
            cut = two if f == 8 else three
            c[f"u{k}h" + tag * (f == 1)] = cut(spread(uh, 0))
            c[f"u{k}l" + tag * (f == 1)] = cut(spread(ul, at_l))

    def tile34(d):
        z = np.zeros((8, 3 * BAND))
        z[0:1, :BAND], z[1:2, :BAND] = block(lows[4], 4, d), block(highs[4], 4, d)
        z[2:4, BAND : 2 * BAND] = block(lows[3], 3, d)
        z[4:6, BAND : 2 * BAND] = block(highs[3], 3, d)
        z[6:8, 2 * BAND :] = block(highs[3], 3, d)
        return z

    def tiles(z, f):
        return np.concatenate([per_field(z[:, i * BAND : (i + 1) * BAND], f) for i in range(3)], axis=1)

    for f, tag in ((8, "m"), (1, "i")):
        out = [tiles(tile34(d), f) for d in (0, 1, -1, 2, -2)]
        for d in (3, -3, 4):
            z = tile34(d)
            assert np.abs(z[2:]).max() == 0
            m = tiles(z[:2], f)
            out.append(m if f == 8 else pad_rows(m, 8))
        assert np.abs(tile34(-4)).max() == 0 and np.abs(tile34(5)).max() == 0 and np.abs(tile34(-5)).max() == 0
        m = np.concatenate(out, axis=0)
        c[f"w{tag}"] = halves(m) if f == 8 else three(m)
    spread = np.kron(np.eye(8), np.eye(8)[:, :2])
    c["x34"] = np.concatenate([spread, spread], axis=1).astype(bf16)

    def pick(k, start, stop, rows_out, low_slots, high_slots):
        n = NROW >> k
        m = inverse_matrix(n)
        m[np.abs(m) < 1e-13] = 0.0
        base = mid * (BAND >> k)
        part = m[base + start : base + stop]
        low, high = part[:, : n // 2], part[:, n // 2 :]
        half = base // 2
        out = np.zeros((rows_out, len(low_slots)))
        seen = 0.0
        for i in range(len(low_slots)):
            if low_slots[i] is not None:
                out[: stop - start, i] += low[:, half + low_slots[i]]
            if high_slots[i] is not None:
                out[: stop - start, i] += high[:, half + high_slots[i]]
        want = (np.abs(low).sum() if any(s is not None for s in low_slots) else 0.0) + (
            np.abs(high).sum() if any(s is not None for s in high_slots) else 0.0
        )
        assert abs(want - np.abs(out).sum()) < 1e-9, k
        return out


    none = [None]
    bands = list(range(-3, 5))
    flat = lambda rows: sum(rows, [])
    l4 = flat([[b] + none * 7 for b in bands])
    h4 = flat([none + [b] + none * 6 for b in bands])
    m4 = pick(4, -2, 6, 8, l4, h4)
    l3 = flat([none * 2 + [2 * b, 2 * b + 1] + none * 4 for b in bands])
    h3 = flat([none * 4 + [2 * b, 2 * b + 1] + none * 2 for b in bands])
    h3l = flat([none * 6 + [2 * b, 2 * b + 1] for b in bands])
    low3 = pick(3, -2, 8, 16, list(range(-2, 6)), none * 8)
    c["s34"] = three(np.concatenate([low3 @ m4, pick(3, -2, 8, 16, none * 64, h3l), pick(3, -2, 8, 16, l3, h3)], axis=0))
    near = (-1, 0, 1)
    l2 = flat([[4 * b + i for i in range(4)] + none * 4 for b in near]) + none * 8
    h2 = flat([none * 4 + [4 * b + i for i in range(4)] for b in near]) + none * 8
    c["s2h"] = three(pick(2, -2, 12, 16, l2, h2))
    low_ext = [-2 + i if i < 10 else None for i in range(16)]
    ha = flat([[4 * b + i for i in range(4)] + none * 4 for b in near]) + none * 8
    hb = flat([none * 4 + [4 * b + i for i in range(4)] for b in near]) + none * 8
    c["s2x"] = three(pick(2, -2, 12, 16, low_ext, none * 16))
    c["s2p"] = three(np.concatenate([pick(2, -2, 12, 16, none * 32, ha), pick(2, -2, 12, 16, none * 32, hb)], axis=0))
    s1 = list(range(8)) + list(range(-4, 0)) + list(range(8, 12))
    c["s1h"] = three(pick(1, -2, 18, 24, s1 + none * 16, none * 16 + s1))
    low_ext = [-2 + i if i < 14 else None for i in range(16)]
    c["s1x"] = three(pick(1, -2, 18, 24, low_ext, none * 16))
    c["s1p"] = three(pick(1, -2, 18, 24, none * 16, s1))
    s0 = inner + edge + [-2, -1, 16, 17] + none * 12
    c["s0h"] = three(pick(0, 0, 32, 32, s0 + none * 32, none * 32 + s0))
    low_ext = [-2 + i if i < 20 else None for i in range(32)]
    c["s0x"] = three(pick(0, 0, 32, 32, low_ext, none * 32))
    c["s0p"] = three(pick(0, 0, 32, 32, none * 32, s0))
    return c


GROUPS = (
    ("bf",),
    ("v0h", "v0l", "b34", "a1h", "a1l", "a2h", "a2l"),
    ("wm",),
    ("a0h", "a0l"),
    ("a0hi", "a0li", "a1hi", "a1li", "a2hi", "a2li", "wi"),
    ("u0h", "u0l", "u1h", "u1l", "u2h", "u2l", "x34", "u0hi", "u0li", "u1hi", "u1li", "u2hi", "u2li"),
    ("i34", "s34", "s2h", "s2x", "s2p", "s1h", "s1x", "s1p", "s0h", "s0x", "s0p"),
    ("bi",),
)


@functools.lru_cache(maxsize=None)
def packed():
    c = constants()
    assert sorted(sum(GROUPS, ())) == sorted(c)
    arrays, where = [], {}
    for g, names in enumerate(GROUPS):
        wide = max(-(-c[n].shape[1] // 128) * 128 for n in names)
        parts, at = [], 0
        for n in names:
            m = c[n]
            tall = -(-m.shape[0] // 16) * 16
            full = np.zeros((tall, wide), bf16)
            full[: m.shape[0], : m.shape[1]] = m
            parts.append(full)
            where[n] = (g, at, m.shape[0], m.shape[1])
            at += tall
        arrays.append(np.concatenate(parts, axis=0))
    return arrays, where


def split(x):
    hi = x.astype(bf16)
    return hi, (x - hi.astype(f32)).astype(bf16)


def dot(a, b):
    return jnp.dot(a, b, preferred_element_type=f32)


def rows(*parts):
    return jnp.concatenate(parts, axis=0)


def lanes(*parts):
    return jnp.concatenate(parts, axis=1) if len(parts) > 1 else parts[0]


COUNT = len(GROUPS)
NEXT, FAR = (1, -1), (2, -2, 3, -3, -4)


def kernel(members_hbm, increment_hbm, weights_hbm, *refs):
    groups_hbm, out, groups = refs[:COUNT], refs[COUNT], refs[COUNT + 1 : 2 * COUNT + 1]
    (members, increment, weights, t_hi, t_lo, b_hi, b_lo, u_hi, u_lo,
     y0e, y1, yc, i0i, i0e, i1, ic,
     hs0, hs1, hs2, hr0, hr1, hr2, gs0, gs1, gs2, gr0, gr1, gr2,
     ks, kr, js, jr, qs, qr, gks, gkr,
     e0i, e0e, e1, ec, ce0i, ce0e, ce1, cec, es0i, es0e, es1, es2, er0i, er0e, er1, er2,
     syc, srt, p0i, p0e, p1, pc, ss0, ss1, sr0, sr1,
     sem_s, sem_r, sem_l) = refs[2 * COUNT + 1 :]
    where = packed()[1]
    mem, tile = lax.axis_index("mem"), lax.axis_index("tile")
    ypos, core = lax.div(mem, 2), lax.rem(mem, 2)

    def at_tile(d):
        return (mem, lax.rem(tile + TILE + d, TILE))

    def at_y(j):
        return (lax.rem(ypos + j, 4) * 2 + core, tile)

    partner = (ypos * 2 + 1 - core, tile)
    near = [at_tile(d) for d in (1, -1, 2, -2, 3, -3, 4, -4)] + [partner] + [at_y(j) for j in (1, 2, 3)]
    barrier = pltpu.get_barrier_semaphore()

    sources = [(groups_hbm[0], groups[0]), (members_hbm, members), (increment_hbm, increment)]
    sources += [(groups_hbm[g], groups[g]) for g in range(1, COUNT)] + [(weights_hbm, weights)]
    loads = [pltpu.make_async_copy(a, b, sem_l.at[n]) for n, (a, b) in enumerate(sources)]
    order = [0] + list(range(3, COUNT + 2))
    begun, loaded = set(), set()

    def begin(*which):
        for n in which:
            loads[n].start()
            begun.add(n)

    def need(n):
        if n not in loaded:
            loads[n].wait()
            loaded.add(n)

    def const(name):
        g, at, tall, wide = where[name]
        need(order[g])
        return groups[g][at : at + tall, :wide]

    def triple(name):
        m = const(name)
        half = m.shape[1] // 2
        return lanes(m[:, :half], m[:, :half], m[:, half:])

    sent = []

    def send(src, dst, device):
        n = len(sent)
        if n == 0:
            pl.semaphore_wait(barrier, len(near))
        copy = pltpu.make_async_remote_copy(
            src_ref=src, dst_ref=dst, send_sem=sem_s.at[n], recv_sem=sem_r.at[n], device_id=device, device_id_type=MESH
        )
        copy.start()
        sent.append(copy)
        return copy

    def window(ref, width, j, first, last):
        start = 256 * j - 128
        groups_ = []
        for t in [(start // 128 + i) % (width // 128) for i in range(4)]:
            if groups_ and groups_[-1][1] == t:
                groups_[-1][1] = t + 1
            else:
                groups_.append([t, t + 1])
        return lanes(*[ref[first:last, 128 * a : 128 * b] for a, b in groups_])

    def put(hi_ref, lo_ref, first, last, width, j, r):
        half = width // 2
        for ref, v in zip((hi_ref, lo_ref), split(r)):
            ref[first:last, 128 * j : 128 * j + 128] = v[:, :128]
            ref[first:last, half + 128 * j : half + 128 * j + 128] = v[:, 128:]

    base = [0, 2048, 3072]
    begin(0, 1)
    for device in near:
        pl.semaphore_signal(barrier, inc=1, device_id=device, device_id_type=MESH)
    bf = const("bf")
    bf_hi, bf_lo = bf[:512], bf[512:]
    need(1)
    begin(3, 4, 2, 5, 6, 7)
    for j in range(8):
        w = window(members, 2048, j, 0, 256)
        r = dot(w, bf_hi) + dot(w, bf_lo)
        put(t_hi, t_lo, 0, 256, 2048, j, r)
        r = r.reshape(8, 32, 256)
        put(b_hi, b_lo, 0, 128, 2048, j, rows(r[:, 24:].reshape(64, 256), r[:, :8].reshape(64, 256)))

    def part(k, which, first, last):
        half = 1024 >> k
        s = base[k] + (half if which == "h" else 0)
        hi, lo = t_hi[first:last, s : s + half], t_lo[first:last, s : s + half]
        return rows(hi, lo, hi)

    owed = {}
    for which, s in (("h", 1024), ("l", 0)):
        hi, lo = b_hi[:, s : s + 1024], b_lo[:, s : s + 1024]
        owed[which] = dot(triple("v0" + which), rows(hi, lo, hi))
    halos = [[], [], []]

    def share(k, h, l, hs, hr):
        half = h.shape[0] // 2
        for n, d in enumerate((1, -1)):
            hs[n] = rows(h[n * half : n * half + half], l[n * half : n * half + half]).astype(bf16)
            halos[k].append(send(hs.at[n], hr.at[n], at_tile(d)))

    share(0, owed["h"], owed["l"], hs0, hr0)

    def down(k, first, last):
        width, s = 2048 >> k, base[k - 1]
        tall, count = last - first, width // 256
        each = 1 if tall > 32 else count
        for j in range(0, count, each):
            a = rows(*[window(t_hi.at[:, s : s + width], width, i, first, last) for i in range(j, j + each)])
            b = rows(*[window(t_lo.at[:, s : s + width], width, i, first, last) for i in range(j, j + each)])
            r = dot(a, bf_hi) + dot(b, bf_hi) + dot(a, bf_lo)
            for i in range(each):
                put(t_hi.at[:, base[k] : base[k] + width], t_lo.at[:, base[k] : base[k] + width], first, last, width, j + i, r[tall * i : tall * i + tall])

    begin(*range(8, COUNT + 3))
    down(1, 0, 256)
    share(1, dot(triple("a1h")[128:], part(1, "h", 0, 256)), dot(triple("a1l")[64:], part(1, "l", 0, 256)), hs1, hr1)
    down(2, 0, 256)

    def stack34(first, last):
        m, s = const("b34"), base[2]
        a, b = t_hi[first:last, s : s + 256], t_lo[first:last, s : s + 256]
        r = dot(a, m[:256]) + dot(b, m[:256]) + dot(a, m[256:])
        hi, lo = split(rows(r[:, :128], r[:, 128:256], r[:, 256:]))
        return rows(hi, lo, hi)

    wm = dot(triple("wm"), stack34(0, 256))
    yc[:, 384:] = wm[0:64]
    far = []
    for n, d in enumerate((1, -1)):
        ks[n] = wm[64 + 64 * n : 128 + 64 * n]
        far.append(send(ks.at[n], kr.at[n], at_tile(d)))
    for n, d in enumerate((2, -2)):
        js[n] = wm[192 + 64 * n : 256 + 64 * n].astype(bf16)
        far.append(send(js.at[n], jr.at[n], at_tile(d)))
    for n, d in enumerate((3, -3, 4)):
        qs[n] = wm[320 + 16 * n : 336 + 16 * n].astype(bf16)
        far.append(send(qs.at[n], qr.at[n], at_tile(d)))

    share(2, dot(triple("a2h")[64:], part(2, "h", 0, 256)), dot(triple("a2l")[128:], part(2, "l", 0, 256)), hs2, hr2)

    y = dot(triple("a0h"), part(0, "h", 0, 256))
    x = dot(triple("a0l"), part(0, "l", 0, 256))
    for n, v in enumerate((y[:64], y[64:128], x[:64])):
        e0i[:, :, :, 1024 * n : 1024 * n + 1024] = (v * v).reshape(4, 2, 8, 1024)
    pair0i = send(e0i.at[:, 1 - core], ce0i, partner)
    y0e[:, 0:1024], y0e[:, 1024:2048], y0e[:, 2048:] = y[128:192], y[192:], x[64:]

    h = dot(triple("a1h")[:128], part(1, "h", 0, 256))
    l = dot(triple("a1l")[:64], part(1, "l", 0, 256))
    y1[:, 0:512], y1[:, 512:1024], y1[:, 1024:] = h[:64], h[64:], l
    h = dot(triple("a2h")[:64], part(2, "h", 0, 256))
    l = dot(triple("a2l")[:128], part(2, "l", 0, 256))
    yc[:, 0:256], yc[:, 256:384] = h, l[:64, :128] + l[64:, 128:]

    need(2)
    hi, lo = split(increment[...])
    u_hi[...], u_lo[...] = hi, lo
    a = rows(*[window(u_hi, 2048, j, 0, 32) for j in range(8)])
    b = rows(*[window(u_lo, 2048, j, 0, 32) for j in range(8)])
    r = dot(rows(a, b), bf_hi)
    r = r[:256] + r[256:] + dot(a, bf_lo)
    for j in range(8):
        put(t_hi, t_lo, 256, 288, 2048, j, r[32 * j : 32 * j + 32])
    for k in (1, 2):
        down(k, 256, 288)
    gifts = [[], [], []]

    def give(k, n8, p8, gs, gr):
        tall = gs.shape[1]
        for n, (d, v) in enumerate(((1, n8), (-1, p8))):
            gs[n] = v[:tall]
            gifts[k].append(send(gs.at[n], gr.at[n], at_tile(d)))

    y = dot(const("a0hi"), part(0, "h", 256, 288))
    x = dot(const("a0li"), part(0, "l", 256, 288))
    give(0, y[32:40] + x[16:24], y[40:48] + x[24:32], gs0, gr0)
    i0i[:, 0:1024], i0i[:, 1024:2048], i0i[:, 2048:] = y[:8], y[8:16], x[:8]
    i0e[:, 0:1024], i0e[:, 1024:2048], i0e[:, 2048:] = y[16:24], y[24:32], x[8:16]
    y = dot(const("a1hi"), part(1, "h", 256, 288))
    x = dot(const("a1li"), part(1, "l", 256, 288))
    give(1, y[16:24] + x[8:16], y[24:32] + x[16:24], gs1, gr1)
    i1[:, 0:512], i1[:, 512:1024], i1[:, 1024:] = y[:8], y[8:16], x[:8]
    y = dot(const("a2hi"), part(2, "h", 256, 288))
    x = dot(const("a2li"), part(2, "l", 256, 288))
    give(2, y[8:16] + x[16:24], y[16:24] + x[24:32], gs2, gr2)
    ic[:, 0:256], ic[:, 256:384] = y[:8], x[:8, :128] + x[8:16, 128:]

    wi = dot(const("wi"), stack34(256, 288))
    ic[:, 384:] = wi[0:8]
    z8 = jnp.zeros((8, 128), f32)
    farther = []
    for n, d in enumerate((1, -1, 2, -2, 3, -3, 4)):
        gks[n] = wi[8 + 8 * n : 16 + 8 * n]
        farther.append(send(gks.at[n], gkr.at[n], at_tile(d)))

    def fold(v):
        half = v.shape[1] // 2
        v = v * v
        return rows(v[:, :half], v[:, half:]).astype(bf16)

    def unfold(v):
        v = jnp.sqrt(v.astype(f32))
        return lanes(v[:8], v[8:])

    def along_y(e, ce, es, er):
        copies = []
        for j in (2, 1, 3):
            q = lax.rem(ypos + j, 4)
            es[j - 1] = fold(e[q, core] + ce[q])
            copies.append(send(es.at[j - 1], er.at[j - 1], at_y(j)))
        return copies

    def total(e, ce, er, copies):
        v = e[ypos, core] + ce[ypos]
        for copy in copies:
            copy.wait_recv()
        return v + unfold(er[0]) + unfold(er[1]) + unfold(er[2])

    pair0i.wait_recv()
    over0i = along_y(e0i, ce0i, es0i, er0i)

    def got(k, ref):
        for copy in halos[k]:
            copy.wait_recv()
        a, b = ref[0], ref[1]
        return rows(a, b, a, b)

    g = got(0, hr0)
    q = dot(const("u0h"), g)
    x = dot(const("u0l"), g)
    for n, v in enumerate((q[:64], q[64:], x)):
        v = v + y0e[:, 1024 * n : 1024 * n + 1024]
        e0e[:, :, :, 1024 * n : 1024 * n + 1024] = (v * v).reshape(4, 2, 8, 1024)
    pair0e = send(e0e.at[:, 1 - core], ce0e, partner)

    g = got(1, hr1)
    q = dot(const("u1h"), g)
    x = dot(const("u1l"), g)
    for n, v in enumerate((q[:64], q[64:], x)):
        v = v + y1[:, 512 * n : 512 * n + 512]
        e1[:, :, :, 512 * n : 512 * n + 512] = (v * v).reshape(4, 2, 8, 512)
    pair1 = send(e1.at[:, 1 - core], ce1, partner)

    g = got(2, hr2)
    v = yc[:, 0:256] + dot(const("u2h"), g)
    ec[:, :, :, 0:256] = (v * v).reshape(4, 2, 8, 256)
    x = dot(const("u2l"), g)
    v = yc[:, 256:384] + x[:64, :128] + x[64:, 128:]
    ec[:, :, :, 256:384] = (v * v).reshape(4, 2, 8, 128)
    pair0e.wait_recv()
    over0e = along_y(e0e, ce0e, es0e, er0e)
    pair1.wait_recv()
    over1 = along_y(e1, ce1, es1, er1)
    for copy in far:
        copy.wait_recv()
    q = qr[0].astype(f32) + qr[1].astype(f32) + qr[2].astype(f32)
    v34 = kr[0] + kr[1] + jr[0].astype(f32) + jr[1].astype(f32) + dot(const("x34"), rows(*split(q)))
    v = yc[:, 384:] + v34
    ec[:, :, :, 384:] = (v * v).reshape(4, 2, 8, 128)
    pairc = send(ec.at[:, 1 - core], cec, partner)
    def taken(k, ref):
        for copy in gifts[k]:
            copy.wait_recv()
        a, b = ref[0], ref[1]
        z = [jnp.zeros((8, a.shape[1]), f32)] * (a.shape[0] == 4)
        hi, lo = split(rows(a, b, *z))
        return rows(hi, lo, hi)

    g = taken(0, gr0)
    q = dot(const("u0hi"), g)
    i0e[:, 0:1024] += q[:8]
    i0e[:, 1024:2048] += q[8:]
    i0e[:, 2048:] += dot(const("u0li"), g)
    g = taken(1, gr1)
    q = dot(const("u1hi"), g)
    i1[:, 0:512] += q[:8]
    i1[:, 512:1024] += q[8:]
    i1[:, 1024:] += dot(const("u1li"), g)
    g = taken(2, gr2)
    ic[:, 0:256] += dot(const("u2hi"), g)
    x = dot(const("u2li"), g)
    ic[:, 256:384] += x[:8, :128] + x[8:, 128:]
    for copy in farther:
        copy.wait_recv()
    v = gkr[0] + gkr[1] + gkr[2] + gkr[3]
    row = lax.broadcasted_iota(jnp.int32, (8, 128), 0)
    ic[:, 384:] += v + jnp.where(row < 2, gkr[4] + gkr[5] + gkr[6], 0.0)
    pairc.wait_recv()
    overc = []
    for j in (2, 1, 3):
        q = lax.rem(ypos + j, 4)
        es2[j - 1] = ec[q, core] + cec[q]
        overc.append(send(es2.at[j - 1], er2.at[j - 1], at_y(j)))

    need(COUNT + 2)
    w = [weights[i] * (1.0 / (MEM - 1)) for i in range(16)]

    def scaled(energy, ref, k):
        third = ref.shape[1] // 3
        return [w[3 * k + j] * energy[:, third * n : third * n + third] * ref[:, third * n : third * n + third] for n, j in enumerate((0, 2, 1))]

    def keep(ref, values):
        third = ref.shape[1] // 3
        for n, v in enumerate(values):
            ref[:, third * n : third * n + third] = v

    keep(p0i, scaled(total(e0i, ce0i, er0i, over0i), i0i, 0))
    keep(p0e, scaled(total(e0e, ce0e, er0e, over0e), i0e, 0))
    ss0[0] = p0e[6:8]
    ss0[1] = p0e[0:2]
    syn0 = [send(ss0.at[n], sr0.at[n], at_tile(d)) for n, d in enumerate((1, -1))]

    keep(p1, scaled(total(e1, ce1, er1, over1), i1, 1))
    ss1[0] = p1[4:8]
    ss1[1] = p1[0:4]
    syn1 = [send(ss1.at[n], sr1.at[n], at_tile(d)) for n, d in enumerate(NEXT)]

    lane = lax.broadcasted_iota(jnp.int32, (8, 128), 1)
    w34 = jnp.where(
        row < 2,
        jnp.where(row == 0, jnp.where(lane < 64, w[15], w[12]), jnp.where(lane < 64, w[13], w[14])),
        jnp.where(row < 4, w[9], jnp.where(row < 6, w[11], w[10])),
    )
    w2 = jnp.where(lax.broadcasted_iota(jnp.int32, (8, 256), 0) < 4, w[6], w[8])
    v = ec[ypos, core] + cec[ypos]
    for copy in overc:
        copy.wait_recv()
    pc[...] = lanes(w2, jnp.full((8, 128), w[7]), w34) * (v + er2[0] + er2[1] + er2[2]) * ic[...]
    sync = [send(pc.at[:, 384:], srt.at[n], at_tile(d)) for n, d in enumerate(FAR)]
    sync += [send(pc, syc.at[n], at_tile(d)) for n, d in enumerate(NEXT)]

    bi = const("bi")
    bi_hi, bi_lo = bi[:768], bi[768:]

    def left(name, x):
        hi, lo = split(x)
        return dot(const(name), rows(hi, lo, hi))

    def columns(x, sides=2):
        tall, half = x.shape[0], x.shape[1] // sides
        count = half // 128
        starts = (0, half)[:sides]

        def win(j):
            return lanes(*[x[:, s + 128 * ((j + i) % count) : s + 128 * ((j + i) % count) + 128] for s in starts for i in (-1, 0, 1)])

        a, b = split(rows(*[win(j) for j in range(count)]))
        r = dot(rows(a, b), bi_hi[: 384 * sides])
        r = r[: tall * count] + r[tall * count :] + dot(a, bi_lo[: 384 * sides])
        return lanes(*[r[tall * j : tall * j + tall] for j in range(count)])

    for copy in syn0:
        copy.wait_recv()
    stack = rows(p0i[...], p0e[...], sr0[0], sr0[1], jnp.zeros((12, 3072), f32))
    out[...] = columns(lanes(left("s0p", stack[:, 2048:]), left("s0h", rows(stack[:, 0:1024], stack[:, 1024:2048]))))
    for copy in syn1:
        copy.wait_recv()
    stack = rows(p1[...], sr1[0], sr1[1])
    base0 = columns(lanes(left("s1p", stack[:, 1024:]), left("s1h", rows(stack[:, 0:512], stack[:, 512:1024]))))

    for copy in sent:
        copy.wait_send()
    for copy in sync:
        copy.wait_recv()
    own, beside = pc[...], [syc[0], syc[1]]
    t = {0: own[:, 384:], -1: beside[0][:, 384:], 1: beside[1][:, 384:]}
    for n, d in enumerate(FAR):
        t[-d] = srt[n]
    x = left("s34", rows(*[t[b] for b in range(-3, 5)]))
    hi, lo = split(lanes(x[:16], x[16:32], x[32:]))
    m = const("i34")
    ll2 = dot(hi, m[:384]) + dot(lo, m[:384]) + dot(hi, m[384:])
    stack = rows(beside[0][:, 0:384], own[:, 0:384], beside[1][:, 0:384], jnp.zeros((8, 384), f32))
    x = left("s2p", stack[:, 256:])
    base1 = columns(lanes(x[:16], x[16:], left("s2h", stack[:, :256])))
    ll1 = base1 + columns(left("s2x", ll2), 1)
    ll0 = base0 + columns(left("s1x", ll1), 1)
    out[...] += columns(left("s0x", rows(ll0, jnp.zeros((8, 1024), f32))), 1)


def local(members, increment, weights):
    arrays = packed()[0]
    anywhere = pl.BlockSpec(memory_space=pl.ANY)
    v = pltpu.VMEM
    scratch = [v(a.shape, bf16) for a in arrays] + [
        v((256, 2048), bf16), v((BAND, 2048), f32), pltpu.SMEM((16,), f32),
        v((288, 3584), bf16), v((288, 3584), bf16), v((128, 2048), bf16), v((128, 2048), bf16), v((32, 2048), bf16), v((32, 2048), bf16),
        v((64, 3072), f32), v((64, 1536), f32), v((64, 512), f32),
        v((8, 3072), f32), v((8, 3072), f32), v((8, 1536), f32), v((8, 512), f32),
        v((2, 32, 1024), bf16), v((2, 48, 512), bf16), v((2, 64, 256), bf16),
        v((2, 32, 1024), bf16), v((2, 48, 512), bf16), v((2, 64, 256), bf16),
        v((2, 4, 1024), f32), v((2, 8, 512), f32), v((2, 8, 256), f32),
        v((2, 4, 1024), f32), v((2, 8, 512), f32), v((2, 8, 256), f32),
        v((2, 64, 128), f32), v((2, 64, 128), f32), v((2, 64, 128), bf16), v((2, 64, 128), bf16), v((3, 16, 128), bf16), v((3, 16, 128), bf16),
        v((7, 8, 128), f32), v((7, 8, 128), f32),
        v((4, 2, 8, 3072), f32), v((4, 2, 8, 3072), f32), v((4, 2, 8, 1536), f32), v((4, 2, 8, 512), f32),
        v((4, 8, 3072), f32), v((4, 8, 3072), f32), v((4, 8, 1536), f32), v((4, 8, 512), f32),
        v((3, 16, 1536), bf16), v((3, 16, 1536), bf16), v((3, 16, 768), bf16), v((3, 8, 512), f32),
        v((3, 16, 1536), bf16), v((3, 16, 1536), bf16), v((3, 16, 768), bf16), v((3, 8, 512), f32),
        v((2, 8, 512), f32), v((5, 8, 128), f32),
        v((8, 3072), f32), v((8, 3072), f32), v((8, 1536), f32), v((8, 512), f32),
        v((2, 2, 3072), f32), v((2, 4, 1536), f32), v((2, 2, 3072), f32), v((2, 4, 1536), f32),
        pltpu.SemaphoreType.DMA((96,)), pltpu.SemaphoreType.DMA((96,)), pltpu.SemaphoreType.DMA((COUNT + 3,)),
    ]
    result = pl.pallas_call(
        kernel,
        out_shape=pltpu.VMEM((BAND, 2048), f32),
        in_specs=[anywhere] * (3 + COUNT),
        out_specs=pl.BlockSpec(memory_space=pltpu.VMEM),
        scratch_shapes=scratch,
        compiler_params=pltpu.CompilerParams(collective_id=0, has_side_effects=True, vmem_limit_bytes=56 * 2**20),
    )(members.reshape(256, 2048), increment.reshape(BAND, 2048), weights, *[jnp.asarray(a) for a in arrays])
    return result.reshape(1, BAND, 2048)


def solution(mesh):
    return jax.shard_map(
        local,
        mesh=mesh,
        in_specs=(P("mem", None, "tile", None), P("mem", "tile", None), P()),
        out_specs=P("mem", "tile", None),
        check_vma=False,
    )
```

```python
import functools

import jax
import jax.numpy as jnp
import numpy as np
from jax import lax
from jax.experimental import pallas as pl
from jax.experimental.pallas import tpu as pltpu
from jax.sharding import PartitionSpec as P

f32, bf16 = jnp.float32, jnp.bfloat16
MESH = pl.DeviceIdType.MESH
LIFT = (-1.586134342059924, -0.052980118572961, 0.882911075530934, 0.443506852043971)
KAPPA = 1.149604398860241
NROW, BAND, LEVELS, MEM, TILE = 1024, 32, 8, 8, 32
RANK = (2, 3, 4)


def forward_matrix(n):
    x = np.eye(n)
    e, o = x[0::2], x[1::2]
    after = lambda v: np.roll(v, -1, 0)
    before = lambda v: np.roll(v, 1, 0)
    o = o + LIFT[0] * (e + after(e))
    e = e + LIFT[1] * (before(o) + o)
    o = o + LIFT[2] * (e + after(e))
    e = e + LIFT[3] * (before(o) + o)
    return e * KAPPA, o / KAPPA


def inverse_matrix(n):
    z = np.eye(n)
    e, o = z[: n // 2] / KAPPA, z[n // 2 :] * KAPPA
    after = lambda v: np.roll(v, -1, 0)
    before = lambda v: np.roll(v, 1, 0)
    e = e - LIFT[3] * (before(o) + o)
    o = o - LIFT[2] * (e + after(e))
    e = e - LIFT[1] * (before(o) + o)
    o = o - LIFT[0] * (e + after(e))
    out = np.zeros((n, n))
    out[0::2], out[1::2] = e, o
    return out


def pieces(m):
    hi = np.asarray(m, np.float32).astype(bf16)
    lo = (np.asarray(m, np.float64) - hi.astype(np.float64)).astype(bf16)
    return hi, lo


def three(m):
    hi, lo = pieces(m)
    return np.concatenate([hi, hi, lo], axis=1)


def two(m):
    hi, lo = pieces(m)
    return np.concatenate([hi, lo], axis=1)


def per_field(m, fields, places=None):
    return np.kron(np.eye(fields), m)


def pad_rows(m, rows):
    return np.concatenate([m, np.zeros((rows - m.shape[0], m.shape[1]))], axis=0)


@functools.lru_cache(maxsize=None)
def constants():
    c = {}
    lows, highs, chain = [], [], np.eye(NROW)
    for k in range(5):
        low, high = forward_matrix(NROW >> k)
        lows.append(low @ chain)
        highs.append(high @ chain)
        chain = lows[-1]
    mid = 16

    def block(mat, k, d):
        r = (BAND >> k) // 2
        m = mat[mid * r : (mid + 1) * r, (mid - d) * BAND : (mid - d + 1) * BAND].copy()
        m[np.abs(m) < 1e-13] = 0.0
        return m

    def halves(m):
        return np.concatenate(pieces(m), axis=1)

    lo2048, hi2048 = forward_matrix(2048)
    bf = np.concatenate([lo2048[512:640, 896:1408], hi2048[512:640, 896:1408]], axis=0).T
    c["bf"] = np.concatenate(pieces(bf), axis=0)
    l256, h256 = forward_matrix(256)
    l128, h128 = forward_matrix(128)
    c["b34"] = np.concatenate(pieces(np.concatenate([l128 @ l256, h128 @ l256, h256, l256], axis=0).T), axis=0)
    s2048 = inverse_matrix(2048)
    bi = np.concatenate([s2048[1024:1280, 384:768], s2048[1024:1280, 1024 + 384 : 1024 + 768]], axis=1).T
    c["bi"] = np.concatenate(pieces(bi), axis=0)
    s256 = inverse_matrix(256).T
    s512 = inverse_matrix(512).T[:256]
    c["i34"] = np.concatenate(pieces(np.concatenate([inverse_matrix(128).T @ s256[:128], s256], axis=0) @ s512), axis=0)

    inner, edge = list(range(4, 12)), [0, 1, 2, 3, 12, 13, 14, 15]
    for k in range(3):
        bl = {d: block(lows[k], k, d) for d in (0, 1, -1)}
        bh = {d: block(highs[k], k, d) for d in (0, 1, -1)}
        r = RANK[k]
        rows_h = 16 >> k
        place = {}
        for part in ("h", "l"):
            for d in (1, -1):
                full = np.concatenate([bl[d], bh[d]], axis=0) if part == "h" else bh[d]
                u, s, vt = np.linalg.svd(full, full_matrices=False)
                assert s[r:].max(initial=0.0) < 1e-12
                keep = s[:r] > 1e-12
                place[part, d] = (u[:, :r] * s[:r] * keep, vt[:r] * keep[:, None])
        top = lambda m: np.concatenate([m, 0 * m], axis=0)
        bot = lambda m: np.concatenate([0 * m, m], axis=0)
        for f, tag in ((8, "m"), (1, "i")):
            width = 8 * 2 * r if f == 8 else (4, 8, 8)[k]

            def sent(part):
                out = []
                for d in (1, -1):
                    v = place[part, d][1]
                    if f == 8:
                        out.append(per_field(v, f))
                    else:
                        out.append(pad_rows(np.concatenate([np.zeros((r if part == "l" else 0, BAND)), v], axis=0), 8))
                return out

            def spread(u, at):
                out = []
                for d in (1, -1):
                    m = np.zeros((u[d].shape[0], width))
                    m[:, at : at + u[d].shape[1]] = u[d]
                    out.append(m)
                m = np.concatenate(out, axis=1)
                if f == 1 and m.shape[1] < 16:
                    m = np.concatenate([m, np.zeros((m.shape[0], 16 - m.shape[1]))], axis=1)
                return m

            at_l = f * r
            if k == 0:
                own_h = [per_field(m[rows_], f) for rows_ in (inner, edge) for m in (bl[0], bh[0])]
                own_l = [per_field(bh[0][rows_], f) for rows_ in (inner, edge)]
                uh = {d: np.concatenate([per_field(place["h", d][0][:16][edge], f), per_field(place["h", d][0][16:][edge], f)], axis=0) for d in (1, -1)}
                ul = {d: per_field(place["l", d][0][edge], f) for d in (1, -1)}
                full_h = {d: place["h", d][0] for d in (1, -1)}
                assert all(np.abs(full_h[d][:16][inner]).max() < 1e-12 and np.abs(full_h[d][16:][inner]).max() < 1e-12 for d in full_h)
            elif k == 1:
                own_h = [per_field(bl[0], f), per_field(bh[0], f)]
                own_l = [per_field(bh[0], f)]
                uh = {d: np.concatenate([per_field(place["h", d][0][:rows_h], f), per_field(place["h", d][0][rows_h:], f)], axis=0) for d in (1, -1)}
                ul = {d: per_field(place["l", d][0], f) for d in (1, -1)}
            else:
                own_h = [per_field(np.concatenate([bl[0], bh[0]], axis=0), f)]
                own_l = [per_field(top(bh[0]), f), per_field(bot(bh[0]), f)]
                uh = {d: per_field(place["h", d][0], f) for d in (1, -1)}
                ul = {d: np.concatenate([per_field(top(place["l", d][0]), f), per_field(bot(place["l", d][0]), f)], axis=0) for d in (1, -1)}
            if k == 0 and f == 8:
                for part in ("h", "l"):
                    n, p = place[part, 1][1], place[part, -1][1]
                    assert np.abs(n[:, :24]).max() < 1e-12 and np.abs(p[:, 8:]).max() < 1e-12
                    n, p = per_field(n[:, 24:], f), per_field(p[:, :8], f)
                    z = np.zeros_like(n)
                    c[f"v0{part}"] = halves(np.concatenate([np.concatenate([n, z], axis=1), np.concatenate([z, p], axis=1)], axis=0))
                c["a0h"], c["a0l"] = halves(np.concatenate(own_h, axis=0)), halves(np.concatenate(own_l, axis=0))
            else:
                cut = halves if f == 8 else three
                c[f"a{k}h" + tag * (f == 1)] = cut(np.concatenate(own_h + sent("h"), axis=0))
                c[f"a{k}l" + tag * (f == 1)] = cut(np.concatenate(own_l + sent("l"), axis=0))
            cut = two if f == 8 else three
            c[f"u{k}h" + tag * (f == 1)] = cut(spread(uh, 0))
            c[f"u{k}l" + tag * (f == 1)] = cut(spread(ul, at_l))

    def tile34(d):
        z = np.zeros((8, 3 * BAND))
        z[0:1, :BAND], z[1:2, :BAND] = block(lows[4], 4, d), block(highs[4], 4, d)
        z[2:4, BAND : 2 * BAND] = block(lows[3], 3, d)
        z[4:6, BAND : 2 * BAND] = block(highs[3], 3, d)
        z[6:8, 2 * BAND :] = block(highs[3], 3, d)
        return z

    def tiles(z, f):
        return np.concatenate([per_field(z[:, i * BAND : (i + 1) * BAND], f) for i in range(3)], axis=1)

    for f, tag in ((8, "m"), (1, "i")):
        out = [tiles(tile34(d), f) for d in (0, 1, -1, 2, -2)]
        for d in (3, -3, 4):
            z = tile34(d)
            assert np.abs(z[2:]).max() == 0
            m = tiles(z[:2], f)
            out.append(m if f == 8 else pad_rows(m, 8))
        assert np.abs(tile34(-4)).max() == 0 and np.abs(tile34(5)).max() == 0 and np.abs(tile34(-5)).max() == 0
        m = np.concatenate(out, axis=0)
        c[f"w{tag}"] = halves(m) if f == 8 else three(m)
    def pick(k, start, stop, rows_out, low_slots, high_slots):
        n = NROW >> k
        m = inverse_matrix(n)
        m[np.abs(m) < 1e-13] = 0.0
        base = mid * (BAND >> k)
        part = m[base + start : base + stop]
        low, high = part[:, : n // 2], part[:, n // 2 :]
        half = base // 2
        out = np.zeros((rows_out, len(low_slots)))
        seen = 0.0
        for i in range(len(low_slots)):
            if low_slots[i] is not None:
                out[: stop - start, i] += low[:, half + low_slots[i]]
            if high_slots[i] is not None:
                out[: stop - start, i] += high[:, half + high_slots[i]]
        want = (np.abs(low).sum() if any(s is not None for s in low_slots) else 0.0) + (
            np.abs(high).sum() if any(s is not None for s in high_slots) else 0.0
        )
        assert abs(want - np.abs(out).sum()) < 1e-9, k
        return out


    none = [None]
    bands = list(range(-3, 5))
    flat = lambda rows: sum(rows, [])
    l4 = flat([[b] + none * 7 for b in bands])
    h4 = flat([none + [b] + none * 6 for b in bands])
    m4 = pick(4, -2, 6, 8, l4, h4)
    l3 = flat([none * 2 + [2 * b, 2 * b + 1] + none * 4 for b in bands])
    h3 = flat([none * 4 + [2 * b, 2 * b + 1] + none * 2 for b in bands])
    h3l = flat([none * 6 + [2 * b, 2 * b + 1] for b in bands])
    low3 = pick(3, -2, 8, 16, list(range(-2, 6)), none * 8)
    low_ext = [-2 + i if i < 10 else None for i in range(16)]
    low2 = pick(2, -2, 12, 16, low_ext, none * 16)
    c["s34"] = three(np.concatenate([low2 @ low3 @ m4, low2 @ pick(3, -2, 8, 16, none * 64, h3l), low2 @ pick(3, -2, 8, 16, l3, h3)], axis=0))
    near = (-1, 0, 1)
    l2 = flat([[4 * b + i for i in range(4)] + none * 4 for b in near]) + none * 8
    h2 = flat([none * 4 + [4 * b + i for i in range(4)] for b in near]) + none * 8
    c["s2h"] = three(pick(2, -2, 12, 16, l2, h2))
    ha = flat([[4 * b + i for i in range(4)] + none * 4 for b in near]) + none * 8
    hb = flat([none * 4 + [4 * b + i for i in range(4)] for b in near]) + none * 8
    c["s2p"] = three(np.concatenate([pick(2, -2, 12, 16, none * 32, ha), pick(2, -2, 12, 16, none * 32, hb)], axis=0))
    s1 = list(range(8)) + list(range(-4, 0)) + list(range(8, 12))
    c["s1h"] = three(pick(1, -2, 18, 24, s1 + none * 16, none * 16 + s1))
    low_ext = [-2 + i if i < 14 else None for i in range(16)]
    c["s1x"] = three(pick(1, -2, 18, 24, low_ext, none * 16))
    c["s1p"] = three(pick(1, -2, 18, 24, none * 16, s1))
    s0 = inner + edge + [-2, -1, 16, 17] + none * 12
    c["s0h"] = three(pick(0, 0, 32, 32, s0 + none * 32, none * 32 + s0))
    low_ext = [-2 + i if i < 20 else None for i in range(32)]
    c["s0x"] = three(pick(0, 0, 32, 32, low_ext, none * 32))
    c["s0p"] = three(pick(0, 0, 32, 32, none * 32, s0))
    return c


GROUPS = (
    ("bf",),
    ("v0h", "v0l", "b34", "a1h", "a1l", "a2h", "a2l"),
    ("wm",),
    ("a0h", "a0l"),
    ("a0hi", "a0li", "a1hi", "a1li", "a2hi", "a2li", "wi"),
    ("u0h", "u0l", "u1h", "u1l", "u2h", "u2l", "u0hi", "u0li", "u1hi", "u1li", "u2hi", "u2li"),
    ("s34", "s2h", "s2p", "s1h", "s1x", "s1p", "s0h", "s0x", "s0p"),
    ("bi",),
    ("i34",),
)


@functools.lru_cache(maxsize=None)
def packed():
    c = constants()
    assert sorted(sum(GROUPS, ())) == sorted(c)
    arrays, where = [], {}
    for g, names in enumerate(GROUPS):
        wide = max(-(-c[n].shape[1] // 128) * 128 for n in names)
        parts, at = [], 0
        for n in names:
            m = c[n]
            tall = -(-m.shape[0] // 16) * 16
            full = np.zeros((tall, wide), bf16)
            full[: m.shape[0], : m.shape[1]] = m
            parts.append(full)
            where[n] = (g, at, m.shape[0], m.shape[1])
            at += tall
        arrays.append(np.concatenate(parts, axis=0))
    return arrays, where


def split(x):
    hi = x.astype(bf16)
    return hi, (x - hi.astype(f32)).astype(bf16)


def dot(a, b):
    return jnp.dot(a, b, preferred_element_type=f32)


def rows(*parts):
    return jnp.concatenate(parts, axis=0)


def lanes(*parts):
    return jnp.concatenate(parts, axis=1) if len(parts) > 1 else parts[0]


COUNT = len(GROUPS)
NEXT, FAR = (1, -1), (2, -2, 3, -3, -4)


def kernel(members_hbm, increment_hbm, weights_hbm, *refs):
    groups_hbm, out, groups = refs[:COUNT], refs[COUNT], refs[COUNT + 1 : 2 * COUNT + 1]
    (members, increment, weights, t_hi, t_lo, b_hi, b_lo, u_hi, u_lo,
     y0e, y1, yc, i0i, i0e, i1, ic,
     hs0, hs1, hs2, hr0, hr1, hr2, gs0, gs1, gs2, gr0, gr1, gr2,
     ks, kr, js, jr, qs, qr, gks, gkr,
     e0i, e0e, e1, ec, ce0i, ce0e, ce1, es0i, es0e, es1, er0i, er0e, er1, er2,
     syc, srt, p0i, p0e, p1, pc, ss0, ss1, sr0, sr1,
     sem_s, sem_r, sem_l) = refs[2 * COUNT + 1 :]
    where = packed()[1]
    mem, tile = lax.axis_index("mem"), lax.axis_index("tile")
    ypos, core = lax.div(mem, 2), lax.rem(mem, 2)

    def at_tile(d):
        return (mem, lax.rem(tile + TILE + d, TILE))

    def at_y(j):
        return (lax.rem(ypos + j, 4) * 2 + core, tile)

    def at_mem(j):
        return (lax.rem(mem + j, MEM), tile)

    partner = (ypos * 2 + 1 - core, tile)
    near = [at_tile(d) for d in (1, -1, 2, -2, 3, -3, 4, -4)] + [at_mem(j) for j in range(1, MEM)]
    barrier = pltpu.get_barrier_semaphore()

    sources = [(groups_hbm[0], groups[0]), (members_hbm, members), (increment_hbm, increment)]
    sources += [(groups_hbm[g], groups[g]) for g in range(1, COUNT)] + [(weights_hbm, weights)]
    loads = [pltpu.make_async_copy(a, b, sem_l.at[n]) for n, (a, b) in enumerate(sources)]
    order = [0] + list(range(3, COUNT + 2))
    begun, loaded = set(), set()

    def begin(*which):
        for n in which:
            loads[n].start()
            begun.add(n)

    def need(n):
        if n not in loaded:
            loads[n].wait()
            loaded.add(n)

    def const(name):
        g, at, tall, wide = where[name]
        need(order[g])
        return groups[g][at : at + tall, :wide]

    def triple(name):
        m = const(name)
        half = m.shape[1] // 2
        return lanes(m[:, :half], m[:, :half], m[:, half:])

    sent = []

    def send(src, dst, device):
        n = len(sent)
        if n == 0:
            pl.semaphore_wait(barrier, len(near))
        copy = pltpu.make_async_remote_copy(
            src_ref=src, dst_ref=dst, send_sem=sem_s.at[n], recv_sem=sem_r.at[n], device_id=device, device_id_type=MESH
        )
        copy.start()
        sent.append(copy)
        return copy

    def window(ref, width, j, first, last):
        start = 256 * j - 128
        groups_ = []
        for t in [(start // 128 + i) % (width // 128) for i in range(4)]:
            if groups_ and groups_[-1][1] == t:
                groups_[-1][1] = t + 1
            else:
                groups_.append([t, t + 1])
        return lanes(*[ref[first:last, 128 * a : 128 * b] for a, b in groups_])

    def put(hi_ref, lo_ref, first, last, width, j, r):
        half = width // 2
        for ref, v in zip((hi_ref, lo_ref), split(r)):
            ref[first:last, 128 * j : 128 * j + 128] = v[:, :128]
            ref[first:last, half + 128 * j : half + 128 * j + 128] = v[:, 128:]

    base = [0, 2048, 3072]
    begin(0, 1)
    for device in near:
        pl.semaphore_signal(barrier, inc=1, device_id=device, device_id_type=MESH)
    bf = const("bf")
    bf_hi, bf_lo = bf[:512], bf[512:]
    need(1)
    begin(3, 4, 2, 5, 6, 7)
    for j in range(8):
        w = window(members, 2048, j, 0, 256)
        r = dot(w, bf_hi) + dot(w, bf_lo)
        put(t_hi, t_lo, 0, 256, 2048, j, r)
        r = r.reshape(8, 32, 256)
        put(b_hi, b_lo, 0, 128, 2048, j, rows(r[:, 24:].reshape(64, 256), r[:, :8].reshape(64, 256)))

    def part(k, which, first, last):
        half = 1024 >> k
        s = base[k] + (half if which == "h" else 0)
        hi, lo = t_hi[first:last, s : s + half], t_lo[first:last, s : s + half]
        return rows(hi, lo, hi)

    owed = {}
    for which, s in (("h", 1024), ("l", 0)):
        hi, lo = b_hi[:, s : s + 1024], b_lo[:, s : s + 1024]
        owed[which] = dot(triple("v0" + which), rows(hi, lo, hi))
    halos = [[], [], []]

    def share(k, h, l, hs, hr):
        half = h.shape[0] // 2
        for n, d in enumerate((1, -1)):
            hs[n] = rows(h[n * half : n * half + half], l[n * half : n * half + half]).astype(bf16)
            halos[k].append(send(hs.at[n], hr.at[n], at_tile(d)))

    share(0, owed["h"], owed["l"], hs0, hr0)

    def down(k, first, last):
        width, s = 2048 >> k, base[k - 1]
        tall, count = last - first, width // 256
        each = 1 if tall > 32 else count
        for j in range(0, count, each):
            a = rows(*[window(t_hi.at[:, s : s + width], width, i, first, last) for i in range(j, j + each)])
            b = rows(*[window(t_lo.at[:, s : s + width], width, i, first, last) for i in range(j, j + each)])
            r = dot(a, bf_hi) + dot(b, bf_hi) + dot(a, bf_lo)
            for i in range(each):
                put(t_hi.at[:, base[k] : base[k] + width], t_lo.at[:, base[k] : base[k] + width], first, last, width, j + i, r[tall * i : tall * i + tall])

    begin(*range(8, COUNT + 3))
    down(1, 0, 256)
    share(1, dot(triple("a1h")[128:], part(1, "h", 0, 256)), dot(triple("a1l")[64:], part(1, "l", 0, 256)), hs1, hr1)
    down(2, 0, 256)

    def stack34(first, last):
        m, s = const("b34"), base[2]
        a, b = t_hi[first:last, s : s + 256], t_lo[first:last, s : s + 256]
        r = dot(a, m[:256]) + dot(b, m[:256]) + dot(a, m[256:])
        hi, lo = split(rows(r[:, :128], r[:, 128:256], r[:, 256:]))
        return rows(hi, lo, hi)

    wm = dot(triple("wm"), stack34(0, 256))
    yc[:, 384:] = wm[0:64]
    far = []
    for n, d in enumerate((1, -1)):
        ks[n] = wm[64 + 64 * n : 128 + 64 * n]
        far.append(send(ks.at[n], kr.at[n], at_tile(d)))
    for n, d in enumerate((2, -2)):
        js[n] = wm[192 + 64 * n : 256 + 64 * n].astype(bf16)
        far.append(send(js.at[n], jr.at[n], at_tile(d)))
    for n, d in enumerate((3, -3, 4)):
        qs[n] = wm[320 + 16 * n : 336 + 16 * n].astype(bf16)
        far.append(send(qs.at[n], qr.at[n], at_tile(d)))

    share(2, dot(triple("a2h")[64:], part(2, "h", 0, 256)), dot(triple("a2l")[128:], part(2, "l", 0, 256)), hs2, hr2)

    y = dot(triple("a0h"), part(0, "h", 0, 256))
    x = dot(triple("a0l"), part(0, "l", 0, 256))
    for n, v in enumerate((y[:64], y[64:128], x[:64])):
        e0i[:, :, :, 1024 * n : 1024 * n + 1024] = (v * v).reshape(4, 2, 8, 1024)
    pair0i = send(e0i.at[:, 1 - core], ce0i, partner)
    y0e[:, 0:1024], y0e[:, 1024:2048], y0e[:, 2048:] = y[128:192], y[192:], x[64:]

    h = dot(triple("a1h")[:128], part(1, "h", 0, 256))
    l = dot(triple("a1l")[:64], part(1, "l", 0, 256))
    y1[:, 0:512], y1[:, 512:1024], y1[:, 1024:] = h[:64], h[64:], l
    h = dot(triple("a2h")[:64], part(2, "h", 0, 256))
    l = dot(triple("a2l")[:128], part(2, "l", 0, 256))
    yc[:, 0:256], yc[:, 256:384] = h, l[:64, :128] + l[64:, 128:]

    need(2)
    hi, lo = split(increment[...])
    u_hi[...], u_lo[...] = hi, lo
    a = rows(*[window(u_hi, 2048, j, 0, 32) for j in range(8)])
    b = rows(*[window(u_lo, 2048, j, 0, 32) for j in range(8)])
    r = dot(rows(a, b), bf_hi)
    r = r[:256] + r[256:] + dot(a, bf_lo)
    for j in range(8):
        put(t_hi, t_lo, 256, 288, 2048, j, r[32 * j : 32 * j + 32])
    for k in (1, 2):
        down(k, 256, 288)
    gifts = [[], [], []]

    def give(k, n8, p8, gs, gr):
        tall = gs.shape[1]
        for n, (d, v) in enumerate(((1, n8), (-1, p8))):
            gs[n] = v[:tall]
            gifts[k].append(send(gs.at[n], gr.at[n], at_tile(d)))

    y = dot(const("a0hi"), part(0, "h", 256, 288))
    x = dot(const("a0li"), part(0, "l", 256, 288))
    give(0, y[32:40] + x[16:24], y[40:48] + x[24:32], gs0, gr0)
    i0i[:, 0:1024], i0i[:, 1024:2048], i0i[:, 2048:] = y[:8], y[8:16], x[:8]
    i0e[:, 0:1024], i0e[:, 1024:2048], i0e[:, 2048:] = y[16:24], y[24:32], x[8:16]
    y = dot(const("a1hi"), part(1, "h", 256, 288))
    x = dot(const("a1li"), part(1, "l", 256, 288))
    give(1, y[16:24] + x[8:16], y[24:32] + x[16:24], gs1, gr1)
    i1[:, 0:512], i1[:, 512:1024], i1[:, 1024:] = y[:8], y[8:16], x[:8]
    y = dot(const("a2hi"), part(2, "h", 256, 288))
    x = dot(const("a2li"), part(2, "l", 256, 288))
    give(2, y[8:16] + x[16:24], y[16:24] + x[24:32], gs2, gr2)
    ic[:, 0:256], ic[:, 256:384] = y[:8], x[:8, :128] + x[8:16, 128:]

    wi = dot(const("wi"), stack34(256, 288))
    ic[:, 384:] = wi[0:8]
    z8 = jnp.zeros((8, 128), f32)
    farther = []
    for n, d in enumerate((1, -1, 2, -2, 3, -3, 4)):
        gks[n] = wi[8 + 8 * n : 16 + 8 * n]
        farther.append(send(gks.at[n], gkr.at[n], at_tile(d)))

    def fold(v):
        half = v.shape[1] // 2
        v = v * v
        return rows(v[:, :half], v[:, half:]).astype(bf16)

    def unfold(v):
        v = jnp.sqrt(v.astype(f32))
        return lanes(v[:8], v[8:])

    def along_y(e, ce, es, er):
        copies = []
        for j in (2, 1, 3):
            q = lax.rem(ypos + j, 4)
            es[j - 1] = fold(e[q, core] + ce[q])
            copies.append(send(es.at[j - 1], er.at[j - 1], at_y(j)))
        return copies

    def total(e, ce, er, copies):
        v = e[ypos, core] + ce[ypos]
        for copy in copies:
            copy.wait_recv()
        return v + unfold(er[0]) + unfold(er[1]) + unfold(er[2])

    pair0i.wait_recv()
    over0i = along_y(e0i, ce0i, es0i, er0i)

    def got(k, ref):
        for copy in halos[k]:
            copy.wait_recv()
        a, b = ref[0], ref[1]
        return rows(a, b, a, b)

    g = got(0, hr0)
    q = dot(const("u0h"), g)
    x = dot(const("u0l"), g)
    for n, v in enumerate((q[:64], q[64:], x)):
        v = v + y0e[:, 1024 * n : 1024 * n + 1024]
        e0e[:, :, :, 1024 * n : 1024 * n + 1024] = (v * v).reshape(4, 2, 8, 1024)
    pair0e = send(e0e.at[:, 1 - core], ce0e, partner)

    g = got(1, hr1)
    q = dot(const("u1h"), g)
    x = dot(const("u1l"), g)
    for n, v in enumerate((q[:64], q[64:], x)):
        v = v + y1[:, 512 * n : 512 * n + 512]
        e1[:, :, :, 512 * n : 512 * n + 512] = (v * v).reshape(4, 2, 8, 512)
    pair1 = send(e1.at[:, 1 - core], ce1, partner)

    g = got(2, hr2)
    v = yc[:, 0:256] + dot(const("u2h"), g)
    ec[:, :, :, 0:256] = (v * v).reshape(4, 2, 8, 256)
    x = dot(const("u2l"), g)
    v = yc[:, 256:384] + x[:64, :128] + x[64:, 128:]
    ec[:, :, :, 256:384] = (v * v).reshape(4, 2, 8, 128)
    pair0e.wait_recv()
    over0e = along_y(e0e, ce0e, es0e, er0e)
    pair1.wait_recv()
    over1 = along_y(e1, ce1, es1, er1)
    for copy in far:
        copy.wait_recv()
    q = qr[0].astype(f32) + qr[1].astype(f32) + qr[2].astype(f32)
    v34 = kr[0] + kr[1] + jr[0].astype(f32) + jr[1].astype(f32)
    yc[:, 384:] += v34
    for n in range(8):
        yc[8 * n : 8 * n + 2, 384:] += q[2 * n : 2 * n + 2]
    v = yc[:, 384:]
    ec[:, :, :, 384:] = (v * v).reshape(4, 2, 8, 128)
    overc = []
    for j in (4, 3, 5, 2, 6, 1, 7):
        owner = lax.rem(mem + j, MEM)
        overc.append(send(ec.at[lax.div(owner, 2), lax.rem(owner, 2)], er2.at[j - 1], at_mem(j)))
    def taken(k, ref):
        for copy in gifts[k]:
            copy.wait_recv()
        a, b = ref[0], ref[1]
        z = [jnp.zeros((8, a.shape[1]), f32)] * (a.shape[0] == 4)
        hi, lo = split(rows(a, b, *z))
        return rows(hi, lo, hi)

    g = taken(0, gr0)
    q = dot(const("u0hi"), g)
    i0e[:, 0:1024] += q[:8]
    i0e[:, 1024:2048] += q[8:]
    i0e[:, 2048:] += dot(const("u0li"), g)
    g = taken(1, gr1)
    q = dot(const("u1hi"), g)
    i1[:, 0:512] += q[:8]
    i1[:, 512:1024] += q[8:]
    i1[:, 1024:] += dot(const("u1li"), g)
    g = taken(2, gr2)
    ic[:, 0:256] += dot(const("u2hi"), g)
    x = dot(const("u2li"), g)
    ic[:, 256:384] += x[:8, :128] + x[8:, 128:]
    for copy in farther:
        copy.wait_recv()
    v = gkr[0] + gkr[1] + gkr[2] + gkr[3]
    row = lax.broadcasted_iota(jnp.int32, (8, 128), 0)
    ic[:, 384:] += v + jnp.where(row < 2, gkr[4] + gkr[5] + gkr[6], 0.0)
    need(COUNT + 2)
    w = [weights[i] * (1.0 / (MEM - 1)) for i in range(16)]

    def scaled(energy, ref, k):
        third = ref.shape[1] // 3
        return [w[3 * k + j] * energy[:, third * n : third * n + third] * ref[:, third * n : third * n + third] for n, j in enumerate((0, 2, 1))]

    def keep(ref, values):
        third = ref.shape[1] // 3
        for n, v in enumerate(values):
            ref[:, third * n : third * n + third] = v

    keep(p0i, scaled(total(e0i, ce0i, er0i, over0i), i0i, 0))
    keep(p0e, scaled(total(e0e, ce0e, er0e, over0e), i0e, 0))
    ss0[0] = p0e[6:8]
    ss0[1] = p0e[0:2]
    syn0 = [send(ss0.at[n], sr0.at[n], at_tile(d)) for n, d in enumerate((1, -1))]

    keep(p1, scaled(total(e1, ce1, er1, over1), i1, 1))
    ss1[0] = p1[4:8]
    ss1[1] = p1[0:4]
    syn1 = [send(ss1.at[n], sr1.at[n], at_tile(d)) for n, d in enumerate(NEXT)]

    lane = lax.broadcasted_iota(jnp.int32, (8, 128), 1)
    w34 = jnp.where(
        row < 2,
        jnp.where(row == 0, jnp.where(lane < 64, w[15], w[12]), jnp.where(lane < 64, w[13], w[14])),
        jnp.where(row < 4, w[9], jnp.where(row < 6, w[11], w[10])),
    )
    w2 = jnp.where(lax.broadcasted_iota(jnp.int32, (8, 256), 0) < 4, w[6], w[8])
    v = ec[ypos, core]
    for copy in overc:
        copy.wait_recv()
    for n in range(MEM - 1):
        v = v + er2[n]
    pc[...] = lanes(w2, jnp.full((8, 128), w[7]), w34) * v * ic[...]
    sync = [send(pc.at[:, 384:], srt.at[n], at_tile(d)) for n, d in enumerate(FAR)]
    sync += [send(pc, syc.at[n], at_tile(d)) for n, d in enumerate(NEXT)]

    bi = const("bi")
    bi_hi, bi_lo = bi[:768], bi[768:]

    def left(name, x):
        hi, lo = split(x)
        return dot(const(name), rows(hi, lo, hi))

    def columns(x, sides=2):
        tall, half = x.shape[0], x.shape[1] // sides
        count = half // 128
        starts = (0, half)[:sides]

        def win(j):
            return lanes(*[x[:, s + 128 * ((j + i) % count) : s + 128 * ((j + i) % count) + 128] for s in starts for i in (-1, 0, 1)])

        a, b = split(rows(*[win(j) for j in range(count)]))
        r = dot(rows(a, b), bi_hi[: 384 * sides])
        r = r[: tall * count] + r[tall * count :] + dot(a, bi_lo[: 384 * sides])
        return lanes(*[r[tall * j : tall * j + tall] for j in range(count)])

    for copy in syn0:
        copy.wait_recv()
    stack = rows(p0i[...], p0e[...], sr0[0], sr0[1], jnp.zeros((12, 3072), f32))
    out[...] = columns(lanes(left("s0p", stack[:, 2048:]), left("s0h", rows(stack[:, 0:1024], stack[:, 1024:2048]))))
    for copy in syn1:
        copy.wait_recv()
    stack = rows(p1[...], sr1[0], sr1[1])
    base0 = columns(lanes(left("s1p", stack[:, 1024:]), left("s1h", rows(stack[:, 0:512], stack[:, 512:1024]))))

    for copy in sent:
        copy.wait_send()
    for copy in sync:
        copy.wait_recv()
    own, beside = pc[...], [syc[0], syc[1]]
    t = {0: own[:, 384:], -1: beside[0][:, 384:], 1: beside[1][:, 384:]}
    for n, d in enumerate(FAR):
        t[-d] = srt[n]
    x = left("s34", rows(*[t[b] for b in range(-3, 5)]))
    hi, lo = split(lanes(x[:16], x[16:32], x[32:]))
    m = const("i34")
    ll1 = dot(hi, m[:384]) + dot(lo, m[:384]) + dot(hi, m[384:])
    stack = rows(beside[0][:, 0:384], own[:, 0:384], beside[1][:, 0:384], jnp.zeros((8, 384), f32))
    x = left("s2p", stack[:, 256:])
    base1 = columns(lanes(x[:16], x[16:], left("s2h", stack[:, :256])))
    ll1 = ll1 + base1
    ll0 = base0 + columns(left("s1x", ll1), 1)
    out[...] += columns(left("s0x", rows(ll0, jnp.zeros((8, 1024), f32))), 1)


def local(members, increment, weights):
    arrays = packed()[0]
    anywhere = pl.BlockSpec(memory_space=pl.ANY)
    v = pltpu.VMEM
    scratch = [v(a.shape, bf16) for a in arrays] + [
        v((256, 2048), bf16), v((BAND, 2048), f32), pltpu.SMEM((16,), f32),
        v((288, 3584), bf16), v((288, 3584), bf16), v((128, 2048), bf16), v((128, 2048), bf16), v((32, 2048), bf16), v((32, 2048), bf16),
        v((64, 3072), f32), v((64, 1536), f32), v((64, 512), f32),
        v((8, 3072), f32), v((8, 3072), f32), v((8, 1536), f32), v((8, 512), f32),
        v((2, 32, 1024), bf16), v((2, 48, 512), bf16), v((2, 64, 256), bf16),
        v((2, 32, 1024), bf16), v((2, 48, 512), bf16), v((2, 64, 256), bf16),
        v((2, 4, 1024), f32), v((2, 8, 512), f32), v((2, 8, 256), f32),
        v((2, 4, 1024), f32), v((2, 8, 512), f32), v((2, 8, 256), f32),
        v((2, 64, 128), f32), v((2, 64, 128), f32), v((2, 64, 128), bf16), v((2, 64, 128), bf16), v((3, 16, 128), bf16), v((3, 16, 128), bf16),
        v((7, 8, 128), f32), v((7, 8, 128), f32),
        v((4, 2, 8, 3072), f32), v((4, 2, 8, 3072), f32), v((4, 2, 8, 1536), f32), v((4, 2, 8, 512), f32),
        v((4, 8, 3072), f32), v((4, 8, 3072), f32), v((4, 8, 1536), f32),
        v((3, 16, 1536), bf16), v((3, 16, 1536), bf16), v((3, 16, 768), bf16),
        v((3, 16, 1536), bf16), v((3, 16, 1536), bf16), v((3, 16, 768), bf16), v((MEM - 1, 8, 512), f32),
        v((2, 8, 512), f32), v((5, 8, 128), f32),
        v((8, 3072), f32), v((8, 3072), f32), v((8, 1536), f32), v((8, 512), f32),
        v((2, 2, 3072), f32), v((2, 4, 1536), f32), v((2, 2, 3072), f32), v((2, 4, 1536), f32),
        pltpu.SemaphoreType.DMA((96,)), pltpu.SemaphoreType.DMA((96,)), pltpu.SemaphoreType.DMA((COUNT + 3,)),
    ]
    result = pl.pallas_call(
        kernel,
        out_shape=pltpu.VMEM((BAND, 2048), f32),
        in_specs=[anywhere] * (3 + COUNT),
        out_specs=pl.BlockSpec(memory_space=pltpu.VMEM),
        scratch_shapes=scratch,
        compiler_params=pltpu.CompilerParams(collective_id=0, has_side_effects=True, vmem_limit_bytes=56 * 2**20),
    )(members.reshape(256, 2048), increment.reshape(BAND, 2048), weights, *[jnp.asarray(a) for a in arrays])
    return result.reshape(1, BAND, 2048)


def solution(mesh):
    return jax.shard_map(
        local,
        mesh=mesh,
        in_specs=(P("mem", None, "tile", None), P("mem", "tile", None), P()),
        out_specs=P("mem", "tile", None),
        check_vma=False,
    )
```
